32 devices in a mesh: group: 2 (over x), shard: 16 (over z, y, core).
Axes of the slice: x: 2, y: 2, z: 4, core: 2. Of those that a mesh axis runs over, the one named last changes fastest.
Arguments:
- inner_embed: float32 [2, 15360, 768], P('group', 'shard'), may hold values from -6 to 6
- outer_embed: float32 [15360, 768], P('shard'), may hold values from -6 to 6
- moment_embed: float32 [15360, 768], P('shard'), may hold values from -6 to 6
- basis: float32 [15360, 64], P('shard'), may hold values from -6 to 6
- inner_attn: float32 [2, 768, 3072], P('group', 'shard'), may hold values from -6 to 6
- outer_attn: float32 [768, 3072], P(None, 'shard'), may hold values from -6 to 6
- moment_attn: float32 [768, 3072], P(None, 'shard'), may hold values from -6 to 6
- inner_norms: float32 [2, 4, 768], P('group', None, 'shard'), may hold values from -6 to 6
- outer_norms: float32 [4, 768], P(None, 'shard'), may hold values from -6 to 6
- moment_norms: float32 [4, 768], P(None, 'shard'), may hold values from -6 to 6
Outputs:
- new_embed: float32 [15360, 768], P('shard')
- new_moment_embed: float32 [15360, 768], P('shard')
- new_attn: float32 [768, 3072], P(None, 'shard')
- new_moment_attn: float32 [768, 3072], P(None, 'shard')
- new_norms: float32 [4, 768], P(None, 'shard')
- new_moment_norms: float32 [4, 768], P(None, 'shard')
- replica_attn: bfloat16 [768, 3072], P('shard')
The draws below stay inside these ranges and needn't reach their ends.
All inputs are finite; a program needn't handle non-finite values.
Results may differ from the reference program's by a relative error of at most 0.0004.
Values may be sent and summed in bfloat16 or wider, within the bound.
No kernel may reach another device: no remote copies, remote signals or barrier semaphores. Data moves between devices by JAX's collectives and lax.ppermute only.
A program may use at most 64 MiB of HBM per device.

```python
import math
import jax
import jax.numpy as jnp
from jax import lax

D = 768
VOCAB = 15360
RANK = 64
NORMS = 4
GROUPS = 2


def block_scale(own_key, dims, pieces, low, largest):
    factor_of, own = 1.0, jax.random.fold_in(own_key, 6)
    for axis_at, blocks in pieces:
        heights = jnp.exp(jax.random.uniform(jax.random.fold_in(own, axis_at), (blocks,), jnp.float32, low / len(pieces), largest / len(pieces)))
        factor_of = factor_of * jnp.repeat(heights, dims[axis_at] // blocks).reshape([-1 if axis == axis_at else 1 for axis in range(len(dims))])
    return factor_of


def gaussian(own_key, shape, scale, most, split=(), kind=jnp.bfloat16):
    result = jax.random.normal(own_key, shape, jnp.float32) * scale
    if len(split) > 0:
        result = block_scale(own_key, shape, split, -0.22, 0.18) * result
    return jnp.clip(result, min=-most, max=most).astype(kind)


def setup_inputs(seed: int = 0) -> dict:
    streams_of = jax.random.split(jax.random.key(seed), 11)
    inner_embed = gaussian(streams_of[0], (GROUPS, VOCAB, D), 1.0, 6.0, ((0, 2), (1, 16)), jnp.float32)
    outer_embed = gaussian(streams_of[1], (VOCAB, D), 1.0, 6.0, ((0, 16),), jnp.float32)
    moment_embed = gaussian(streams_of[2], (VOCAB, D), 1.0, 6.0, ((0, 16),), jnp.float32)
    basis = gaussian(streams_of[3], (VOCAB, RANK), 1.0, 6.0, ((0, 16),), jnp.float32)
    inner_attn = gaussian(streams_of[4], (GROUPS, D, 4 * D), 1.0, 6.0, ((0, 2), (1, 16)), jnp.float32)
    outer_attn = gaussian(streams_of[5], (D, 4 * D), 1.0, 6.0, ((1, 16),), jnp.float32)
    moment_attn = gaussian(streams_of[6], (D, 4 * D), 1.0, 6.0, ((1, 16),), jnp.float32)
    inner_norms = gaussian(streams_of[7], (GROUPS, NORMS, D), 1.0, 6.0, ((0, 2), (2, 16)), jnp.float32)
    outer_norms = gaussian(streams_of[8], (NORMS, D), 1.0, 6.0, ((1, 16),), jnp.float32)
    moment_norms = gaussian(streams_of[9], (NORMS, D), 1.0, 6.0, ((1, 16),), jnp.float32)
    return dict(inner_embed=inner_embed, outer_embed=outer_embed, moment_embed=moment_embed, basis=basis, inner_attn=inner_attn, outer_attn=outer_attn, moment_attn=moment_attn, inner_norms=inner_norms, outer_norms=outer_norms, moment_norms=moment_norms)


def nesterov(outer, moment, delta):
    moment_new = 0.5 * moment + delta
    return (outer - (delta + 0.5 * moment_new), moment_new)

def reference(inner_embed, outer_embed, moment_embed, basis, inner_attn, outer_attn, moment_attn, inner_norms, outer_norms, moment_norms):
    coefficient = jnp.zeros((RANK, D), jnp.float32)
    for index in range(GROUPS):
        differ = outer_embed - inner_embed[index]
        coefficient = coefficient + jnp.dot(basis.T, differ, precision=lax.Precision.HIGHEST, preferred_element_type=jnp.float32)
    coefficient = coefficient / GROUPS
    embed_delta = jnp.dot(basis, coefficient, precision=lax.Precision.HIGHEST, preferred_element_type=jnp.float32) * (1.0 / math.sqrt(RANK * VOCAB))
    attn_delta = lax.optimization_barrier(jnp.mean(outer_attn[None] - inner_attn, axis=0))
    norm_delta = lax.optimization_barrier(jnp.mean(outer_norms[None] - inner_norms, axis=0))
    new_embed, new_moment_embed = nesterov(outer_embed, moment_embed, embed_delta)
    new_attn, new_moment_attn = nesterov(outer_attn, moment_attn, attn_delta)
    new_norms, new_moment_norms = nesterov(outer_norms, moment_norms, norm_delta)
    replica_attn = new_attn.astype(jnp.bfloat16)
    return (new_embed, new_moment_embed, new_attn, new_moment_attn, new_norms, new_moment_norms, replica_attn)
```

```python
import functools
import math

import jax
import jax.numpy as jnp
from jax import lax
from jax.experimental import pallas as pl
from jax.experimental.pallas import tpu as pltpu
from jax.sharding import PartitionSpec as P

VOCAB = 15360
RANK = 64
LANES = 128
HALF = 64
ROWS = 40

f32 = jnp.float32
bf16 = jnp.bfloat16
VMEM = pltpu.VMEM
LIMIT = 40 * 1024 * 1024


def nesterov(outer, moment, delta):
    moment_new = 0.5 * moment + delta
    return (outer - (delta + 0.5 * moment_new), moment_new)


def remote(count):
    return [pl.BlockSpec(memory_space=pltpu.HBM)] * count


def cost(flops, moved):
    return pl.CostEstimate(flops=flops, bytes_accessed=moved, transcendentals=0)


def left_half(shape):
    return lax.broadcasted_iota(jnp.int32, shape, 1) < HALF


def roll_half(x):
    return pltpu.roll(x, HALF, 1)


def split3(x):
    hi = x.astype(bf16)
    lo = (x - hi.astype(f32)).astype(bf16)
    return hi, lo


def dot3(a, b, dims):
    ah, al = split3(a)
    bh, bl = split3(b)
    mul = functools.partial(lax.dot_general, dimension_numbers=(dims, ((), ())), preferred_element_type=f32)
    return mul(ah, bh) + (mul(ah, bl) + mul(al, bh))


def chunks(rows):
    return [(at, min(256, rows - at)) for at in range(0, rows, 256)]


def coeff_kernel(basis_in, outer_in, inner_in, mine_ref, other_ref, basis_ref, outer_ref, inner_ref, sems):
    parts = chunks(outer_ref.shape[0])

    def copy(src, dst, at, size, sem):
        return pltpu.make_async_copy(src.at[pl.ds(at, size)], dst.at[pl.ds(at, size)], sems.at[sem])

    copies = [copy(basis_in, basis_ref, 0, basis_ref.shape[0], 0)]
    for k, (at, size) in enumerate(parts):
        copies.append(copy(outer_in, outer_ref, at, size, 1 + 2 * k))
        copies.append(copy(inner_in, inner_ref, at, size, 2 + 2 * k))
    for c in copies:
        c.start()
    copies[0].wait()
    first = lax.rem(lax.axis_index("shard"), 2) == 0
    rows = mine_ref.shape[0]
    total = None
    for k, (at, size) in enumerate(parts):
        copies[1 + 2 * k].wait()
        copies[2 + 2 * k].wait()
        part = slice(at, at + size)
        term = dot3(basis_ref[:, part], outer_ref[part, :] - inner_ref[part, :], ((1,), (0,)))
        total = term if total is None else total + term
    low, high = total[:rows], total[rows:]
    other_ref[...] = jnp.where(first, high, low)
    mine_ref[...] = jnp.where(first, low, high)


def norm_tile(scr, norm_ref):
    scr[...] = jnp.zeros_like(scr)
    scr[: norm_ref.shape[0], : norm_ref.shape[1]] = norm_ref[...]
    return roll_half(scr[...])


def make_piece(main, half, tile):
    mask = left_half((8, LANES))
    third = jnp.where(mask, half[0:8], roll_half(half[8:16]))
    return jnp.concatenate([main, third, jnp.where(mask, half[16:24], tile)], axis=0)


def put_piece(out_ref, at, main, half, tile):
    out_ref[at] = make_piece(main, half, tile)


def get_half(piece):
    return jnp.concatenate([piece[24:32], roll_half(piece[24:32]), piece[32:40]], axis=0)


def pack_kernel(shards, load, store, x_ref, norm_ref, out_ref, scr):
    load(1)
    tile = norm_tile(scr, norm_ref)
    mask = left_half((24, LANES))
    for group in range(2):
        load(0, group)
        rows = slice(24 * group, 24 * group + 24)
        for pair in range(shards // 2):
            at = group * shards + 2 * pair
            t = [x_ref[rows, 384 * pair + LANES * k : 384 * pair + LANES * k + LANES] for k in range(3)]
            t1, t2 = roll_half(t[1]), roll_half(t[2])
            put_piece(out_ref, at, t[0], t[1], tile)
            put_piece(out_ref, at + 1, jnp.where(mask, t1, t2), t2, tile)
        store(0, slice(group * shards, group * shards + shards))


def states_kernel(shards, load, store, outer_ref, moment_ref, outer_norm_ref, moment_norm_ref, outer_out, moment_out, scr, tile_scr):
    group = lax.axis_index("group")
    for n, (src, norm, out) in enumerate(((outer_ref, outer_norm_ref, outer_out), (moment_ref, moment_norm_ref, moment_out))):
        load(2 + n)
        tile = norm_tile(tile_scr, norm)
        load(n)
        for k in range(src.shape[1] // LANES):
            cols = slice(LANES * k, LANES * k + LANES)
            scr[n, cols, 0:LANES] = src[0:LANES, cols].T
            scr[n, cols, LANES : LANES + HALF] = src[LANES : LANES + HALF, cols].T
        for s in range(shards):
            rows = pl.ds(pl.multiple_of(48 * s + 24 * group, 8), 24)
            out[s] = make_piece(scr[n, rows, :LANES], scr[n, rows, LANES:], tile)
        store(n)


def middle_kernel(shards, load, store, outer_ref, moment_ref, got_ref, send_ref, delta_ref):
    for n in range(3):
        load(n)
    for s in range(shards):
        outer = outer_ref[s]
        delta = ((outer - got_ref[s]) + (outer - got_ref[shards + s])) * 0.5
        delta_ref[s] = delta
        new = nesterov(outer, moment_ref[s], delta)[0].astype(bf16)
        send_ref[s] = new
        send_ref[shards + s] = new
    store(0)
    store(1)


def last_kernel(shards, scale, embed, load, store, *refs):
    n_in = len(LAST_IN)
    r = dict(zip(LAST_IN + LAST_OUT, refs))
    scr = refs[len(r)]
    at_in = {name: n for n, name in enumerate(LAST_IN)}
    at_out = {name: n for n, name in enumerate(LAST_OUT)}
    group, me = lax.axis_index("group"), lax.axis_index("shard")
    for name in ("coeff_mine", "coeff_other", "basis"):
        load(at_in[name])
    first = lax.rem(me, 2) == 0
    mine, other = r["coeff_mine"][...], r["coeff_other"][...]
    coeff = jnp.concatenate([jnp.where(first, mine, other), jnp.where(first, other, mine)], axis=0) * scale
    for k, (at, size) in enumerate(embed):
        part = slice(at, at + size)
        delta = dot3(r["basis"][:, part], coeff, ((0,), (0,)))
        load(at_in["outer_embed"], k)
        load(at_in["moment_embed"], k)
        r["new_embed"][part, :], r["new_moment_embed"][part, :] = nesterov(
            r["outer_embed"][part, :], r["moment_embed"][part, :], delta
        )
        store(at_out["new_embed"], part)
        store(at_out["new_moment_embed"], part)
    load(at_in["got"])
    mask = left_half((24, LANES))
    for pair in range(shards // 2):
        tiles = [[], [], []]
        for g in range(2):
            even, odd = (r["got"][g * shards + 2 * pair + n].astype(f32) for n in range(2))
            turned = roll_half(odd[0:24])
            tiles[0].append(even[0:24])
            tiles[1].append(jnp.where(mask, get_half(even), turned))
            tiles[2].append(jnp.where(mask, turned, roll_half(get_half(odd))))
        for k in range(3):
            at = 384 * pair + LANES * k
            r["replica"][:, at : at + LANES] = jnp.concatenate(tiles[k], axis=0).astype(bf16)
    store(at_out["replica"])
    for name, owner in (("delta_mine", group), ("delta_other", 1 - group)):
        load(at_in[name])
        for s in range(shards):
            piece = r[name][s]
            rows = pl.ds(pl.multiple_of(48 * s + 24 * owner, 8), 24)
            scr[rows, 0:LANES] = piece[0:24]
            scr[rows, LANES : 2 * LANES] = get_half(piece)
    for name in ("outer_attn", "moment_attn", "outer_norms", "moment_norms"):
        load(at_in[name])
    for k in range(r["outer_attn"].shape[1] // LANES):
        cols = slice(LANES * k, LANES * k + LANES)
        for rows, part in ((slice(0, LANES), scr[cols, 0:LANES].T), (slice(LANES, LANES + HALF), scr[cols, LANES : 2 * LANES].T[:HALF])):
            r["new_attn"][rows, cols], r["new_moment_attn"][rows, cols] = nesterov(
                r["outer_attn"][rows, cols], r["moment_attn"][rows, cols], part
            )
    store(at_out["new_attn"])
    store(at_out["new_moment_attn"])
    tile = roll_half(r["delta_mine"][me, 32:40, :])
    norms, width = r["outer_norms"].shape
    r["new_norms"][...], r["new_moment_norms"][...] = nesterov(
        r["outer_norms"][...], r["moment_norms"][...], tile[:norms, :width]
    )
    store(at_out["new_norms"])
    store(at_out["new_moment_norms"])


LAST_IN = (
    "coeff_mine", "coeff_other", "basis", "outer_embed", "moment_embed", "got", "delta_mine", "delta_other",
    "outer_attn", "moment_attn", "outer_norms", "moment_norms",
)
LAST_OUT = ("new_embed", "new_moment_embed", "new_attn", "new_moment_attn", "new_norms", "new_moment_norms", "replica")


def staged(kernel, parts, count, *refs):
    ins, outs = refs[: len(parts)], refs[len(parts) : count]
    scratch = list(refs[count:])
    held_in = [scratch.pop(0) if p else ref for p, ref in zip(parts, ins, strict=True)]
    held_out = [scratch.pop(0) for _ in outs]
    in_sem, out_sem = scratch.pop(0), scratch.pop(0)

    def copy(n, k):
        at, size = parts[n][k]
        part = slice(at, at + size)
        return pltpu.make_async_copy(ins[n].at[part], held_in[n].at[part], in_sem.at[sum(len(p) for p in parts[:n]) + k])

    for k in range(max(len(p) for p in parts)):
        for n in range(len(parts)):
            if k < len(parts[n]):
                copy(n, k).start()

    def load(n, k=0):
        if parts[n]:
            copy(n, k).wait()

    def store(n, part=slice(None)):
        pltpu.make_async_copy(held_out[n].at[part], outs[n].at[part], out_sem.at[n]).start()

    kernel(load, store, *held_in, *held_out, *scratch)
    for n in range(len(outs)):
        pltpu.make_async_copy(held_out[n], outs[n], out_sem.at[n]).wait()


def call(kernel, args, outs, scratch=(), flops=0, parts=None, here=()):
    moved = sum(x.size * x.dtype.itemsize for x in args) + sum(math.prod(s) * jnp.dtype(d).itemsize for s, d in outs)
    parts = parts or {}
    parts = [[] if n in here else parts.get(n, [(0, x.shape[0])]) for n, x in enumerate(args)]
    return pl.pallas_call(
        functools.partial(staged, kernel, parts, len(args) + len(outs)),
        out_shape=[pltpu.HBM(s, d) for s, d in outs],
        in_specs=[pl.BlockSpec(memory_space=pltpu.HBM if p else VMEM) for p in parts],
        out_specs=remote(len(outs)),
        scratch_shapes=[pltpu.VMEM(x.shape, x.dtype) for x, p in zip(args, parts, strict=True) if p]
        + [pltpu.VMEM(s, d) for s, d in outs]
        + [pltpu.SemaphoreType.DMA((sum(len(p) for p in parts),)), pltpu.SemaphoreType.DMA((len(outs),))]
        + list(scratch),
        compiler_params=pltpu.CompilerParams(vmem_limit_bytes=LIMIT),
        cost_estimate=cost(flops, moved),
    )(*[pltpu.with_memory_space_constraint(x, pltpu.HBM) if p else x for x, p in zip(args, parts, strict=True)])


def after(x, *others):
    return lax.optimization_barrier((x, *others))[0]


def everyone(x):
    return lax.all_to_all(x, ("group", "shard"), split_axis=0, concat_axis=0, tiled=True)


def swap_groups(x):
    return lax.ppermute(x, "group", [(0, 1), (1, 0)])


def swap_shards(x, bit):
    return lax.ppermute(x, "shard", [(i, i ^ bit) for i in range(lax.axis_size("shard"))])


def fast(
    inner_embed, outer_embed, moment_embed, basis, inner_attn, outer_attn, moment_attn,
    inner_norms, outer_norms, moment_norms,
):
    shards = lax.axis_size("shard")
    rows, width = outer_embed.shape
    rank = basis.shape[1]
    basis = basis.T
    outer_attn, moment_attn = outer_attn.T, moment_attn.T
    piece = (shards, ROWS, LANES)

    (sent,) = call(
        functools.partial(pack_kernel, shards), (inner_attn[0], inner_norms[0]), [((2 * shards, ROWS, LANES), f32)],
        [pltpu.VMEM((8, LANES), f32)], parts={0: [(0, 24), (24, 24)]},
    )
    got = everyone(sent)

    mine, other = pl.pallas_call(
        coeff_kernel,
        out_shape=[jax.ShapeDtypeStruct((rank // 2, width), f32)] * 2,
        in_specs=remote(3),
        out_specs=[pl.BlockSpec(memory_space=VMEM)] * 2,
        scratch_shapes=[pltpu.VMEM(basis.shape, f32)]
        + [pltpu.VMEM(outer_embed.shape, f32)] * 2
        + [pltpu.SemaphoreType.DMA((1 + 2 * len(chunks(rows)),))],
        compiler_params=pltpu.CompilerParams(vmem_limit_bytes=LIMIT),
        cost_estimate=cost(6 * rank * rows * width, 8 * rows * width),
    )(*[pltpu.with_memory_space_constraint(x, pltpu.HBM) for x in (basis, outer_embed, inner_embed[0])])
    mine = mine + swap_shards(other, 1)
    steps = [mine]
    mine = mine + swap_groups(mine)
    steps.append(mine)
    bit = 2
    while bit < shards:
        mine = mine + swap_shards(mine, bit)
        steps.append(mine)
        bit *= 2
    other = swap_shards(mine, 1)

    outer_piece, moment_piece = call(
        functools.partial(states_kernel, shards), (outer_attn, moment_attn, outer_norms, moment_norms), [(piece, f32)] * 2,
        [pltpu.VMEM((2, outer_attn.shape[1], 2 * LANES), f32), pltpu.VMEM((8, LANES), f32)],
    )
    send, delta = call(
        functools.partial(middle_kernel, shards), (after(outer_piece, steps[2]), moment_piece, got),
        [((2 * shards, ROWS, LANES), bf16), (piece, f32)], here=(2,),
    )
    replica = everyone(send)
    delta_other = swap_groups(delta)
    embed = chunks(rows)
    new_embed, new_moment_embed, new_attn, new_moment_attn, new_norms, new_moment_norms, replica_attn = call(
        functools.partial(last_kernel, shards, 0.5 / math.sqrt(RANK * VOCAB), embed),
        (mine, other, basis, outer_embed, moment_embed, replica, delta, delta_other, outer_attn, moment_attn, outer_norms, moment_norms),
        [((rows, width), f32)] * 2 + [(outer_attn.shape, f32)] * 2 + [(outer_norms.shape, f32)] * 2 + [(inner_attn.shape[1:], bf16)],
        [pltpu.VMEM((outer_attn.shape[1], 2 * LANES), f32)], flops=6 * rank * rows * width, parts={3: embed, 4: embed}, here=(0, 1, 5, 7),
    )
    return (new_embed, new_moment_embed, new_attn.T, new_moment_attn.T, new_norms, new_moment_norms, replica_attn)


def plain(
    inner_embed, outer_embed, moment_embed, basis, inner_attn, outer_attn, moment_attn,
    inner_norms, outer_norms, moment_norms,
):
    groups = lax.axis_size("group")
    coeff = lax.dot_general(
        basis, outer_embed - inner_embed[0], (((0,), (0,)), ((), ())),
        precision=lax.Precision.HIGHEST, preferred_element_type=f32,
    )
    moved = lax.all_to_all(inner_attn[0], "shard", split_axis=1, concat_axis=0, tiled=True)
    coeff = lax.psum(coeff, ("group", "shard")) / groups
    attn_sum, norm_sum = lax.psum((outer_attn - moved, outer_norms - inner_norms[0]), "group")
    embed_delta = jnp.dot(basis, coeff, precision=lax.Precision.HIGHEST, preferred_element_type=f32) * (
        1.0 / math.sqrt(RANK * VOCAB)
    )
    new_embed, new_moment_embed = nesterov(outer_embed, moment_embed, embed_delta)
    new_attn, new_moment_attn = nesterov(outer_attn, moment_attn, attn_sum / groups)
    new_norms, new_moment_norms = nesterov(outer_norms, moment_norms, norm_sum / groups)
    replica_attn = lax.all_to_all(new_attn.astype(bf16), "shard", split_axis=0, concat_axis=1, tiled=True)
    return (new_embed, new_moment_embed, new_attn, new_moment_attn, new_norms, new_moment_norms, replica_attn)


def on_device(*args):
    outer_embed, basis, inner_attn, outer_attn, norms = args[1], args[3], args[4], args[5], args[8]
    shards = lax.axis_size("shard")
    fits = (
        lax.axis_size("group") == 2
        and shards >= 2
        and shards & (shards - 1) == 0
        and inner_attn.shape == (1, 48, 192 * shards)
        and outer_attn.shape == (48 * shards, 192)
        and outer_attn.shape[0] % LANES == 0
        and norms.shape[0] <= 8
        and norms.shape[1] <= HALF
        and outer_embed.shape[1] % 256 == 0
        and outer_embed.shape[0] % 8 == 0
        and basis.shape[1] % 16 == 0
    )
    return (fast if fits else plain)(*args)


def solution(mesh):
    placed = (
        P("group", "shard", None),
        P("shard", None),
        P("shard", None),
        P("shard", None),
        P("group", "shard", None),
        P(None, "shard"),
        P(None, "shard"),
        P("group", None, "shard"),
        P(None, "shard"),
        P(None, "shard"),
    )
    return jax.shard_map(
        on_device,
        mesh=mesh,
        in_specs=placed,
        out_specs=(
            P("shard", None),
            P("shard", None),
            P(None, "shard"),
            P(None, "shard"),
            P(None, "shard"),
            P(None, "shard"),
            P("shard", None),
        ),
        check_vma=False,
    )
```

```python
import functools
import math

import jax
import jax.numpy as jnp
from jax import lax
from jax.experimental import pallas as pl
from jax.experimental.pallas import tpu as pltpu
from jax.sharding import PartitionSpec as P

VOCAB = 15360
RANK = 64
LANES = 128
HALF = 64
ROWS = 40

f32 = jnp.float32
bf16 = jnp.bfloat16
VMEM = pltpu.VMEM
LIMIT = 40 * 1024 * 1024


def nesterov(outer, moment, delta):
    moment_new = 0.5 * moment + delta
    return (outer - (delta + 0.5 * moment_new), moment_new)


def remote(count):
    return [pl.BlockSpec(memory_space=pltpu.HBM)] * count


def cost(flops, moved):
    return pl.CostEstimate(flops=flops, bytes_accessed=moved, transcendentals=0)


def left_half(shape):
    return lax.broadcasted_iota(jnp.int32, shape, 1) < HALF


def roll_half(x):
    return pltpu.roll(x, HALF, 1)


def split3(x):
    hi = x.astype(bf16)
    lo = (x - hi.astype(f32)).astype(bf16)
    return hi, lo


def dot3(a, b):
    rows = a.shape[0]
    ah, al = split3(a)
    bh, bl = split3(b)
    both = jnp.dot(jnp.concatenate([ah, al], axis=0), bh, preferred_element_type=f32)
    return both[:rows] + (both[rows:] + jnp.dot(ah, bl, preferred_element_type=f32))


def chunks(rows):
    return [(at, min(256, rows - at)) for at in range(0, rows, 256)]


def coeff_kernel(basis_in, outer_in, inner_in, mine_ref, other_ref, basis_ref, outer_ref, inner_ref, sems):
    parts = chunks(outer_ref.shape[0])

    def copy(src, dst, at, size, sem):
        return pltpu.make_async_copy(src.at[pl.ds(at, size)], dst.at[pl.ds(at, size)], sems.at[sem])

    copies = [copy(basis_in, basis_ref, 0, basis_ref.shape[0], 0)]
    for k, (at, size) in enumerate(parts):
        copies.append(copy(outer_in, outer_ref, at, size, 1 + 2 * k))
        copies.append(copy(inner_in, inner_ref, at, size, 2 + 2 * k))
    for c in copies:
        c.start()
    copies[0].wait()
    first = lax.rem(lax.axis_index("shard"), 2) == 0
    rows = mine_ref.shape[0]
    total = None
    for k, (at, size) in enumerate(parts):
        copies[1 + 2 * k].wait()
        copies[2 + 2 * k].wait()
        part = slice(at, at + size)
        term = dot3(basis_ref[:, part], outer_ref[part, :] - inner_ref[part, :])
        total = term if total is None else total + term
    low, high = total[:rows], total[rows:]
    other_ref[...] = jnp.where(first, high, low)
    mine_ref[...] = jnp.where(first, low, high)


def norm_tile(scr, norm_ref):
    scr[...] = jnp.zeros_like(scr)
    scr[: norm_ref.shape[0], : norm_ref.shape[1]] = norm_ref[...]
    return roll_half(scr[...])


def make_piece(main, half, tile):
    mask = left_half((8, LANES))
    third = jnp.where(mask, half[0:8], roll_half(half[8:16]))
    return jnp.concatenate([main, third, jnp.where(mask, half[16:24], tile)], axis=0)


def put_piece(out_ref, at, main, half, tile):
    out_ref[at] = make_piece(main, half, tile)


def get_half(piece):
    return jnp.concatenate([piece[24:32], roll_half(piece[24:32]), piece[32:40]], axis=0)


def pack_kernel(shards, load, store, x_ref, norm_ref, out_ref, scr):
    load(1)
    tile = norm_tile(scr, norm_ref)
    mask = left_half((24, LANES))
    for group in range(2):
        load(0, group)
        rows = slice(24 * group, 24 * group + 24)
        for pair in range(shards // 2):
            at = group * shards + 2 * pair
            t = [x_ref[rows, 384 * pair + LANES * k : 384 * pair + LANES * k + LANES] for k in range(3)]
            t1, t2 = roll_half(t[1]), roll_half(t[2])
            put_piece(out_ref, at, t[0], t[1], tile)
            put_piece(out_ref, at + 1, jnp.where(mask, t1, t2), t2, tile)
        store(0, slice(group * shards, group * shards + shards))


def states_kernel(shards, load, store, outer_ref, moment_ref, outer_norm_ref, moment_norm_ref, outer_out, moment_out, scr, tile_scr):
    group = lax.axis_index("group")
    for n, (src, norm, out) in enumerate(((outer_ref, outer_norm_ref, outer_out), (moment_ref, moment_norm_ref, moment_out))):
        load(2 + n)
        tile = norm_tile(tile_scr, norm)
        load(n)
        for k in range(src.shape[1] // LANES):
            cols = slice(LANES * k, LANES * k + LANES)
            scr[n, cols, 0:LANES] = src[0:LANES, cols].T
            scr[n, cols, LANES : LANES + HALF] = src[LANES : LANES + HALF, cols].T
        for s in range(shards):
            rows = pl.ds(pl.multiple_of(48 * s + 24 * group, 8), 24)
            out[s] = make_piece(scr[n, rows, :LANES], scr[n, rows, LANES:], tile)
        store(n)


def middle_kernel(shards, load, store, outer_ref, moment_ref, got_ref, send_ref, delta_ref):
    for n in range(3):
        load(n)
    for s in range(shards):
        outer = outer_ref[s]
        delta = ((outer - got_ref[s]) + (outer - got_ref[shards + s])) * 0.5
        delta_ref[s] = delta
        new = nesterov(outer, moment_ref[s], delta)[0].astype(bf16)
        send_ref[s] = new
        send_ref[shards + s] = new
    store(0)
    store(1)


def join_kernel(scale, mine_ref, other_ref, out_ref):
    first = lax.rem(lax.axis_index("shard"), 2) == 0
    mine, other = mine_ref[...] * scale, other_ref[...] * scale
    high, low = split3(jnp.concatenate([jnp.where(first, mine, other), jnp.where(first, other, mine)], axis=0))
    out_ref[...] = jnp.concatenate([high, low, high], axis=0)


def embed_kernel(parts, load, store, coeff_ref, basis_ref, outer_ref, moment_ref, new_ref, new_moment_ref):
    coeff = coeff_ref[...]
    load(1)
    for k, (at, size) in enumerate(parts):
        part = slice(at, at + size)
        high, low = split3(basis_ref[:, part])
        three = jnp.concatenate([high, high, low], axis=0)
        delta = lax.dot_general(three, coeff, (((0,), (0,)), ((), ())), preferred_element_type=f32)
        load(2, k)
        load(3, k)
        new_ref[part, :], new_moment_ref[part, :] = nesterov(outer_ref[part, :], moment_ref[part, :], delta)
        store(0, part)
        store(1, part)


def replica_kernel(shards, load, store, got_ref, out_ref):
    mask = left_half((24, LANES))
    for pair in range(shards // 2):
        tiles = [[], [], []]
        for g in range(2):
            even, odd = (got_ref[g * shards + 2 * pair + n].astype(f32) for n in range(2))
            turned = roll_half(odd[0:24])
            tiles[0].append(even[0:24])
            tiles[1].append(jnp.where(mask, get_half(even), turned))
            tiles[2].append(jnp.where(mask, turned, roll_half(get_half(odd))))
        for k in range(3):
            at = 384 * pair + LANES * k
            out_ref[:, at : at + LANES] = jnp.concatenate(tiles[k], axis=0).astype(bf16)
        if pair % 2:
            store(0, (slice(None), slice(384 * pair - 384, 384 * pair + 384)))


def attn_kernel(
    shards, load, store, mine_ref, other_ref, outer_ref, moment_ref, outer_norm_ref, moment_norm_ref,
    new_ref, new_moment_ref, new_norm_ref, new_moment_norm_ref, scr,
):
    group, me = lax.axis_index("group"), lax.axis_index("shard")
    for n, (src, owner) in enumerate(((mine_ref, group), (other_ref, 1 - group))):
        load(n)
        for s in range(shards):
            piece = src[s]
            rows = pl.ds(pl.multiple_of(48 * s + 24 * owner, 8), 24)
            scr[rows, 0:LANES] = piece[0:24]
            scr[rows, LANES : 2 * LANES] = get_half(piece)
    for n in range(2, 6):
        load(n)
    for k in range(outer_ref.shape[1] // LANES):
        cols = slice(LANES * k, LANES * k + LANES)
        for rows, part in ((slice(0, LANES), scr[cols, 0:LANES].T), (slice(LANES, LANES + HALF), scr[cols, LANES : 2 * LANES].T[:HALF])):
            new_ref[rows, cols], new_moment_ref[rows, cols] = nesterov(outer_ref[rows, cols], moment_ref[rows, cols], part)
    store(0)
    store(1)
    tile = roll_half(mine_ref[me, 32:40, :])
    norms, width = outer_norm_ref.shape
    new_norm_ref[...], new_moment_norm_ref[...] = nesterov(
        outer_norm_ref[...], moment_norm_ref[...], tile[:norms, :width]
    )
    store(2)
    store(3)


def staged(kernel, parts, count, *refs):
    ins, outs = refs[: len(parts)], refs[len(parts) : count]
    scratch = list(refs[count:])
    held_in = [scratch.pop(0) if p else ref for p, ref in zip(parts, ins, strict=True)]
    held_out = [scratch.pop(0) for _ in outs]
    in_sem, out_sem = scratch.pop(0), scratch.pop(0)

    def copy(n, k):
        at, size = parts[n][k]
        part = slice(at, at + size)
        return pltpu.make_async_copy(ins[n].at[part], held_in[n].at[part], in_sem.at[sum(len(p) for p in parts[:n]) + k])

    for k in range(max(len(p) for p in parts)):
        for n in range(len(parts)):
            if k < len(parts[n]):
                copy(n, k).start()

    def load(n, k=0):
        if parts[n]:
            copy(n, k).wait()

    def store(n, part=slice(None)):
        pltpu.make_async_copy(held_out[n].at[part], outs[n].at[part], out_sem.at[n]).start()

    kernel(load, store, *held_in, *held_out, *scratch)
    for n in range(len(outs)):
        pltpu.make_async_copy(held_out[n], outs[n], out_sem.at[n]).wait()


def call(kernel, args, outs, scratch=(), flops=0, parts=None, here=(), weight=1):
    moved = sum(x.size * x.dtype.itemsize for x in args) + sum(math.prod(s) * jnp.dtype(d).itemsize for s, d in outs)
    parts = parts or {}
    parts = [[] if n in here else parts.get(n, [(0, x.shape[0])]) for n, x in enumerate(args)]
    return pl.pallas_call(
        functools.partial(staged, kernel, parts, len(args) + len(outs)),
        out_shape=[pltpu.HBM(s, d) for s, d in outs],
        in_specs=[pl.BlockSpec(memory_space=pltpu.HBM if p else VMEM) for p in parts],
        out_specs=remote(len(outs)),
        scratch_shapes=[pltpu.VMEM(x.shape, x.dtype) for x, p in zip(args, parts, strict=True) if p]
        + [pltpu.VMEM(s, d) for s, d in outs]
        + [pltpu.SemaphoreType.DMA((max(1, sum(len(p) for p in parts)),)), pltpu.SemaphoreType.DMA((len(outs),))]
        + list(scratch),
        compiler_params=pltpu.CompilerParams(vmem_limit_bytes=LIMIT),
        cost_estimate=cost(weight * flops, weight * moved),
    )(*[pltpu.with_memory_space_constraint(x, pltpu.HBM) if p else x for x, p in zip(args, parts, strict=True)])


def after(x, *others):
    return lax.optimization_barrier((x, *others))[0]


def everyone(x):
    return lax.all_to_all(x, ("group", "shard"), split_axis=0, concat_axis=0, tiled=True)


def swap_groups(x):
    return lax.ppermute(x, "group", [(0, 1), (1, 0)])


def swap_shards(x, bit):
    return lax.ppermute(x, "shard", [(i, i ^ bit) for i in range(lax.axis_size("shard"))])


def fast(
    inner_embed, outer_embed, moment_embed, basis, inner_attn, outer_attn, moment_attn,
    inner_norms, outer_norms, moment_norms,
):
    shards = lax.axis_size("shard")
    rows, width = outer_embed.shape
    rank = basis.shape[1]
    basis = basis.T
    outer_attn, moment_attn = outer_attn.T, moment_attn.T
    piece = (shards, ROWS, LANES)

    (sent,) = call(
        functools.partial(pack_kernel, shards), (inner_attn[0], inner_norms[0]), [((2 * shards, ROWS, LANES), f32)],
        [pltpu.VMEM((8, LANES), f32)], parts={0: [(0, 24), (24, 24)]},
    )
    got = everyone(sent)

    mine, other = pl.pallas_call(
        coeff_kernel,
        out_shape=[jax.ShapeDtypeStruct((rank // 2, width), f32)] * 2,
        in_specs=remote(3),
        out_specs=[pl.BlockSpec(memory_space=VMEM)] * 2,
        scratch_shapes=[pltpu.VMEM(basis.shape, f32)]
        + [pltpu.VMEM(outer_embed.shape, f32)] * 2
        + [pltpu.SemaphoreType.DMA((1 + 2 * len(chunks(rows)),))],
        compiler_params=pltpu.CompilerParams(vmem_limit_bytes=LIMIT),
        cost_estimate=cost(6 * rank * rows * width, 8 * rows * width),
    )(*[pltpu.with_memory_space_constraint(x, pltpu.HBM) for x in (basis, outer_embed, inner_embed[0])])
    mine = mine + swap_shards(other, 1)
    outer_piece, moment_piece = call(
        functools.partial(states_kernel, shards), (outer_attn, moment_attn, outer_norms, moment_norms), [(piece, f32)] * 2,
        [pltpu.VMEM((2, outer_attn.shape[1], 2 * LANES), f32), pltpu.VMEM((8, LANES), f32)],
    )
    steps = []
    for n, step in enumerate(("x", 4, 8, 2)):
        moved = swap_groups(mine) if step == "x" else swap_shards(mine, step)
        if n == 0:
            moved = after(moved, outer_piece)
        if n == 2:
            send, delta = call(
                functools.partial(middle_kernel, shards), (after(outer_piece, steps[1]), moment_piece, got),
                [((2 * shards, ROWS, LANES), bf16), (piece, f32)], here=(2,),
            )
            moved = after(moved, delta)
        mine = mine + moved
        steps.append(mine)
    other = swap_shards(mine, 1)

    replica = everyone(after(send, steps[2]))
    delta_other = swap_groups(delta)
    embed = chunks(rows)
    coeff = pl.pallas_call(
        functools.partial(join_kernel, 0.5 / math.sqrt(RANK * VOCAB)),
        out_shape=jax.ShapeDtypeStruct((3 * rank, width), bf16),
        in_specs=[pl.BlockSpec(memory_space=VMEM)] * 2,
        out_specs=pl.BlockSpec(memory_space=VMEM),
        compiler_params=pltpu.CompilerParams(vmem_limit_bytes=LIMIT),
        cost_estimate=cost(5 * 10**8, 16 * rank * width),
    )(mine, other)
    new_embed, new_moment_embed = call(
        functools.partial(embed_kernel, embed),
        (after(coeff, delta_other), basis, outer_embed, moment_embed), [((rows, width), f32)] * 2,
        flops=6 * rank * rows * width, parts={2: embed, 3: embed}, here=(0,), weight=18,
    )
    new_attn, new_moment_attn, new_norms, new_moment_norms = call(
        functools.partial(attn_kernel, shards),
        (delta, delta_other, outer_attn, moment_attn, outer_norms, moment_norms),
        [(outer_attn.shape, f32)] * 2 + [(outer_norms.shape, f32)] * 2,
        [pltpu.VMEM((outer_attn.shape[1], 2 * LANES), f32)], here=(1,),
    )
    (replica_attn,) = call(
        functools.partial(replica_kernel, shards), (replica,), [(inner_attn.shape[1:], bf16)], here=(0,)
    )
    return (new_embed, new_moment_embed, new_attn.T, new_moment_attn.T, new_norms, new_moment_norms, replica_attn)


def plain(
    inner_embed, outer_embed, moment_embed, basis, inner_attn, outer_attn, moment_attn,
    inner_norms, outer_norms, moment_norms,
):
    groups = lax.axis_size("group")
    coeff = lax.dot_general(
        basis, outer_embed - inner_embed[0], (((0,), (0,)), ((), ())),
        precision=lax.Precision.HIGHEST, preferred_element_type=f32,
    )
    moved = lax.all_to_all(inner_attn[0], "shard", split_axis=1, concat_axis=0, tiled=True)
    coeff = lax.psum(coeff, ("group", "shard")) / groups
    attn_sum, norm_sum = lax.psum((outer_attn - moved, outer_norms - inner_norms[0]), "group")
    embed_delta = jnp.dot(basis, coeff, precision=lax.Precision.HIGHEST, preferred_element_type=f32) * (
        1.0 / math.sqrt(RANK * VOCAB)
    )
    new_embed, new_moment_embed = nesterov(outer_embed, moment_embed, embed_delta)
    new_attn, new_moment_attn = nesterov(outer_attn, moment_attn, attn_sum / groups)
    new_norms, new_moment_norms = nesterov(outer_norms, moment_norms, norm_sum / groups)
    replica_attn = lax.all_to_all(new_attn.astype(bf16), "shard", split_axis=0, concat_axis=1, tiled=True)
    return (new_embed, new_moment_embed, new_attn, new_moment_attn, new_norms, new_moment_norms, replica_attn)


def on_device(*args):
    outer_embed, basis, inner_attn, outer_attn, norms = args[1], args[3], args[4], args[5], args[8]
    shards = lax.axis_size("shard")
    fits = (
        lax.axis_size("group") == 2
        and shards >= 2
        and shards & (shards - 1) == 0
        and inner_attn.shape == (1, 48, 192 * shards)
        and outer_attn.shape == (48 * shards, 192)
        and outer_attn.shape[0] % LANES == 0
        and shards % 4 == 0
        and norms.shape[0] <= 8
        and norms.shape[1] <= HALF
        and outer_embed.shape[1] % 256 == 0
        and outer_embed.shape[0] % 8 == 0
        and basis.shape[1] % 16 == 0
    )
    return (fast if fits else plain)(*args)


def solution(mesh):
    placed = (
        P("group", "shard", None),
        P("shard", None),
        P("shard", None),
        P("shard", None),
        P("group", "shard", None),
        P(None, "shard"),
        P(None, "shard"),
        P("group", None, "shard"),
        P(None, "shard"),
        P(None, "shard"),
    )
    return jax.shard_map(
        on_device,
        mesh=mesh,
        in_specs=placed,
        out_specs=(
            P("shard", None),
            P("shard", None),
            P(None, "shard"),
            P(None, "shard"),
            P(None, "shard"),
            P(None, "shard"),
            P("shard", None),
        ),
        check_vma=False,
    )
```

```python
import functools
import math

import jax
import jax.numpy as jnp
from jax import lax
from jax.experimental import pallas as pl
from jax.experimental.pallas import tpu as pltpu
from jax.sharding import PartitionSpec as P

VOCAB = 15360
RANK = 64
LANES = 128
HALF = 64
ROWS = 40

f32 = jnp.float32
bf16 = jnp.bfloat16
VMEM = pltpu.VMEM
LIMIT = 40 * 1024 * 1024


def nesterov(outer, moment, delta):
    moment_new = 0.5 * moment + delta
    return (outer - (delta + 0.5 * moment_new), moment_new)


def remote(count):
    return [pl.BlockSpec(memory_space=pltpu.HBM)] * count


def cost(flops, moved):
    return pl.CostEstimate(flops=flops, bytes_accessed=moved, transcendentals=0)


def left_half(shape):
    return lax.broadcasted_iota(jnp.int32, shape, 1) < HALF


def roll_half(x):
    return pltpu.roll(x, HALF, 1)


def split3(x):
    hi = x.astype(bf16)
    lo = (x - hi.astype(f32)).astype(bf16)
    return hi, lo


def dot3(a, b):
    rows = a.shape[0]
    ah, al = split3(a)
    bh, bl = split3(b)
    both = jnp.dot(jnp.concatenate([ah, al], axis=0), bh, preferred_element_type=f32)
    return both[:rows] + (both[rows:] + jnp.dot(ah, bl, preferred_element_type=f32))


def chunks(rows):
    return [(at, min(256, rows - at)) for at in range(0, rows, 256)]


def coeff_kernel(basis_in, outer_in, inner_in, mine_ref, other_ref, basis_ref, outer_ref, inner_ref, sems):
    parts = chunks(outer_ref.shape[0])

    def copy(src, dst, at, size, sem):
        return pltpu.make_async_copy(src.at[pl.ds(at, size)], dst.at[pl.ds(at, size)], sems.at[sem])

    copies = [copy(basis_in, basis_ref, 0, basis_ref.shape[0], 0)]
    for k, (at, size) in enumerate(parts):
        copies.append(copy(outer_in, outer_ref, at, size, 1 + 2 * k))
        copies.append(copy(inner_in, inner_ref, at, size, 2 + 2 * k))
    for c in copies:
        c.start()
    copies[0].wait()
    first = lax.rem(lax.axis_index("shard"), 2) == 0
    rows = mine_ref.shape[0]
    total = None
    for k, (at, size) in enumerate(parts):
        copies[1 + 2 * k].wait()
        copies[2 + 2 * k].wait()
        part = slice(at, at + size)
        term = dot3(basis_ref[:, part], outer_ref[part, :] - inner_ref[part, :])
        total = term if total is None else total + term
    low, high = total[:rows], total[rows:]
    other_ref[...] = jnp.where(first, high, low)
    mine_ref[...] = jnp.where(first, low, high)


def norm_tile(scr, norm_ref):
    scr[...] = jnp.zeros_like(scr)
    scr[: norm_ref.shape[0], : norm_ref.shape[1]] = norm_ref[...]
    return roll_half(scr[...])


def make_piece(main, half, tile):
    mask = left_half((8, LANES))
    third = jnp.where(mask, half[0:8], roll_half(half[8:16]))
    return jnp.concatenate([main, third, jnp.where(mask, half[16:24], tile)], axis=0)


def put_piece(out_ref, at, main, half, tile):
    out_ref[at] = make_piece(main, half, tile)


def get_half(piece):
    return jnp.concatenate([piece[24:32], roll_half(piece[24:32]), piece[32:40]], axis=0)


def put_dense(out_ref, at, main, half):
    mask = left_half((4, LANES))
    for k in range(6):
        out_ref[at, :, LANES * k : LANES * k + LANES] = main[4 * k : 4 * k + 4]
    turned = roll_half(half)
    for k in range(3):
        group = jnp.where(mask, half[8 * k : 8 * k + 4], turned[8 * k + 4 : 8 * k + 8])
        out_ref[at, :, LANES * (6 + k) : LANES * (7 + k)] = group


def get_dense(ref, at):
    groups = [ref[at, :, LANES * k : LANES * k + LANES] for k in range(9)]
    tiles = [jnp.concatenate([g, roll_half(g)], axis=0) for g in groups[6:]]
    third = jnp.where(left_half((8, LANES)), tiles[0], roll_half(tiles[1]))
    return jnp.concatenate(groups[:6] + [third, tiles[2]], axis=0)


def pack_kernel(shards, load, store, x_ref, out_ref):
    mask = left_half((24, LANES))
    for group in range(2):
        load(0, group)
        rows = slice(24 * group, 24 * group + 24)
        for pair in range(shards // 2):
            at = group * shards + 2 * pair
            t = [x_ref[rows, 384 * pair + LANES * k : 384 * pair + LANES * k + LANES] for k in range(3)]
            t1, t2 = roll_half(t[1]), roll_half(t[2])
            put_dense(out_ref, at, t[0], t[1])
            put_dense(out_ref, at + 1, jnp.where(mask, t1, t2), t2)
        store(0, slice(group * shards, group * shards + shards))


def states_kernel(shards, load, store, outer_ref, moment_ref, outer_out, moment_out, scr):
    group = lax.axis_index("group")
    for n, (src, out) in enumerate(((outer_ref, outer_out), (moment_ref, moment_out))):
        load(n)
        for k in range(src.shape[1] // LANES):
            cols = slice(LANES * k, LANES * k + LANES)
            scr[n, cols, 0:LANES] = src[0:LANES, cols].T
            scr[n, cols, LANES : LANES + HALF] = src[LANES : LANES + HALF, cols].T
        for s in range(shards):
            rows = pl.ds(pl.multiple_of(48 * s + 24 * group, 8), 24)
            half = scr[n, rows, LANES:]
            out[s] = make_piece(scr[n, rows, :LANES], half, half[16:24])
        store(n)


def middle_kernel(shards, load, store, outer_ref, moment_ref, norm_ref, got_ref, send_ref, delta_ref, scr):
    for n in (2, 0, 1):
        load(n)
    tile = norm_tile(scr, norm_ref)
    mask = left_half((8, LANES))
    for s in range(shards):
        outer = outer_ref[s]
        delta = ((outer - get_dense(got_ref, s)) + (outer - get_dense(got_ref, shards + s))) * 0.5
        delta_ref[s, 0:32] = delta[0:32]
        delta_ref[s, 32:40] = jnp.where(mask, delta[32:40], tile)
        new = nesterov(outer, moment_ref[s], delta)[0].astype(bf16)
        send_ref[s] = new
        send_ref[shards + s] = new
    store(0)
    store(1)


def join_kernel(scale, mine_ref, other_ref, out_ref):
    first = lax.rem(lax.axis_index("shard"), 2) == 0
    mine, other = mine_ref[...] * scale, other_ref[...] * scale
    high, low = split3(jnp.concatenate([jnp.where(first, mine, other), jnp.where(first, other, mine)], axis=0))
    out_ref[...] = jnp.concatenate([high, low, high], axis=0)


def embed_kernel(parts, load, store, coeff_ref, basis_ref, outer_ref, moment_ref, new_ref, new_moment_ref):
    coeff = coeff_ref[...]
    load(1)
    for k, (at, size) in enumerate(parts):
        part = slice(at, at + size)
        high, low = split3(basis_ref[:, part])
        three = jnp.concatenate([high, high, low], axis=0)
        delta = lax.dot_general(three, coeff, (((0,), (0,)), ((), ())), preferred_element_type=f32)
        load(2, k)
        load(3, k)
        new_ref[part, :], new_moment_ref[part, :] = nesterov(outer_ref[part, :], moment_ref[part, :], delta)
        store(0, part)
        store(1, part)


def replica_kernel(shards, load, store, got_ref, out_ref):
    mask = left_half((24, LANES))
    for pair in range(shards // 2):
        tiles = [[], [], []]
        for g in range(2):
            even, odd = (got_ref[g * shards + 2 * pair + n].astype(f32) for n in range(2))
            turned = roll_half(odd[0:24])
            tiles[0].append(even[0:24])
            tiles[1].append(jnp.where(mask, get_half(even), turned))
            tiles[2].append(jnp.where(mask, turned, roll_half(get_half(odd))))
        for k in range(3):
            at = 384 * pair + LANES * k
            out_ref[:, at : at + LANES] = jnp.concatenate(tiles[k], axis=0).astype(bf16)
        if pair % 2:
            store(0, (slice(None), slice(384 * pair - 384, 384 * pair + 384)))


def attn_kernel(
    shards, load, store, mine_ref, other_ref, outer_ref, moment_ref, outer_norm_ref, moment_norm_ref,
    new_ref, new_moment_ref, new_norm_ref, new_moment_norm_ref, scr,
):
    group = lax.axis_index("group")
    for n, (src, owner) in enumerate(((mine_ref, group), (other_ref, 1 - group))):
        load(n)
        for s in range(shards):
            piece = src[s]
            rows = pl.ds(pl.multiple_of(48 * s + 24 * owner, 8), 24)
            scr[rows, 0:LANES] = piece[0:24]
            scr[rows, LANES : 2 * LANES] = get_half(piece)
    for n in range(2, 6):
        load(n)
    for k in range(outer_ref.shape[1] // LANES):
        cols = slice(LANES * k, LANES * k + LANES)
        for rows, part in ((slice(0, LANES), scr[cols, 0:LANES].T), (slice(LANES, LANES + HALF), scr[cols, LANES : 2 * LANES].T[:HALF])):
            new_ref[rows, cols], new_moment_ref[rows, cols] = nesterov(outer_ref[rows, cols], moment_ref[rows, cols], part)
    store(0)
    store(1)
    norms, width = outer_norm_ref.shape
    outer = outer_norm_ref[...]
    mine, other = (roll_half(ref[0, 32:40, :])[:norms, :width] for ref in (mine_ref, other_ref))
    delta = ((outer - mine) + (outer - other)) * 0.5
    new_norm_ref[...], new_moment_norm_ref[...] = nesterov(outer, moment_norm_ref[...], delta)
    store(2)
    store(3)


def staged(kernel, parts, count, *refs):
    ins, outs = refs[: len(parts)], refs[len(parts) : count]
    scratch = list(refs[count:])
    held_in = [scratch.pop(0) if p else ref for p, ref in zip(parts, ins, strict=True)]
    held_out = [scratch.pop(0) for _ in outs]
    in_sem, out_sem = scratch.pop(0), scratch.pop(0)

    def copy(n, k):
        at, size = parts[n][k]
        part = slice(at, at + size)
        return pltpu.make_async_copy(ins[n].at[part], held_in[n].at[part], in_sem.at[sum(len(p) for p in parts[:n]) + k])

    for k in range(max(len(p) for p in parts)):
        for n in range(len(parts)):
            if k < len(parts[n]):
                copy(n, k).start()

    def load(n, k=0):
        if parts[n]:
            copy(n, k).wait()

    def store(n, part=slice(None)):
        pltpu.make_async_copy(held_out[n].at[part], outs[n].at[part], out_sem.at[n]).start()

    kernel(load, store, *held_in, *held_out, *scratch)
    for n in range(len(outs)):
        pltpu.make_async_copy(held_out[n], outs[n], out_sem.at[n]).wait()


def call(kernel, args, outs, scratch=(), flops=0, parts=None, here=(), weight=1):
    moved = sum(x.size * x.dtype.itemsize for x in args) + sum(math.prod(s) * jnp.dtype(d).itemsize for s, d in outs)
    parts = parts or {}
    parts = [[] if n in here else parts.get(n, [(0, x.shape[0])]) for n, x in enumerate(args)]
    return pl.pallas_call(
        functools.partial(staged, kernel, parts, len(args) + len(outs)),
        out_shape=[pltpu.HBM(s, d) for s, d in outs],
        in_specs=[pl.BlockSpec(memory_space=pltpu.HBM if p else VMEM) for p in parts],
        out_specs=remote(len(outs)),
        scratch_shapes=[pltpu.VMEM(x.shape, x.dtype) for x, p in zip(args, parts, strict=True) if p]
        + [pltpu.VMEM(s, d) for s, d in outs]
        + [pltpu.SemaphoreType.DMA((max(1, sum(len(p) for p in parts)),)), pltpu.SemaphoreType.DMA((len(outs),))]
        + list(scratch),
        compiler_params=pltpu.CompilerParams(vmem_limit_bytes=LIMIT),
        cost_estimate=cost(weight * flops, weight * moved),
    )(*[pltpu.with_memory_space_constraint(x, pltpu.HBM) if p else x for x, p in zip(args, parts, strict=True)])


def after(x, *others):
    return lax.optimization_barrier((x, *others))[0]


def everyone(x):
    return lax.all_to_all(x, ("group", "shard"), split_axis=0, concat_axis=0, tiled=True)


def swap_groups(x):
    return lax.ppermute(x, "group", [(0, 1), (1, 0)])


def swap_shards(x, bit):
    return lax.ppermute(x, "shard", [(i, i ^ bit) for i in range(lax.axis_size("shard"))])


def fast(
    inner_embed, outer_embed, moment_embed, basis, inner_attn, outer_attn, moment_attn,
    inner_norms, outer_norms, moment_norms,
):
    shards = lax.axis_size("shard")
    rows, width = outer_embed.shape
    rank = basis.shape[1]
    basis = basis.T
    outer_attn, moment_attn = outer_attn.T, moment_attn.T
    piece = (shards, ROWS, LANES)

    (sent,) = call(
        functools.partial(pack_kernel, shards), (inner_attn[0],), [((2 * shards, 4, 9 * LANES), f32)],
        parts={0: [(0, 24), (24, 24)]},
    )
    got = everyone(sent)

    mine, other = pl.pallas_call(
        coeff_kernel,
        out_shape=[jax.ShapeDtypeStruct((rank // 2, width), f32)] * 2,
        in_specs=remote(3),
        out_specs=[pl.BlockSpec(memory_space=VMEM)] * 2,
        scratch_shapes=[pltpu.VMEM(basis.shape, f32)]
        + [pltpu.VMEM(outer_embed.shape, f32)] * 2
        + [pltpu.SemaphoreType.DMA((1 + 2 * len(chunks(rows)),))],
        compiler_params=pltpu.CompilerParams(vmem_limit_bytes=LIMIT),
        cost_estimate=cost(6 * rank * rows * width, 8 * rows * width),
    )(*[pltpu.with_memory_space_constraint(x, pltpu.HBM) for x in (basis, outer_embed, inner_embed[0])])
    mine = mine + swap_shards(other, 1)
    outer_piece, moment_piece = call(
        functools.partial(states_kernel, shards), (outer_attn, moment_attn), [(piece, f32)] * 2,
        [pltpu.VMEM((2, outer_attn.shape[1], 2 * LANES), f32)],
    )
    steps = []
    for n, step in enumerate(("x", 2, 4, 8)):
        moved = swap_groups(mine) if step == "x" else swap_shards(mine, step)
        if n == 0:
            moved = after(moved, outer_piece)
        if n == 2:
            send, delta = call(
                functools.partial(middle_kernel, shards), (after(outer_piece, steps[1]), moment_piece, inner_norms[0], got),
                [((2 * shards, ROWS, LANES), bf16), (piece, f32)], [pltpu.VMEM((8, LANES), f32)], here=(3,),
            )
            moved = after(moved, delta)
        mine = mine + moved
        steps.append(mine)
    other = swap_shards(mine, 1)

    replica = everyone(after(send, steps[2]))
    delta_other = swap_groups(delta)
    embed = chunks(rows)
    coeff = pl.pallas_call(
        functools.partial(join_kernel, 0.5 / math.sqrt(RANK * VOCAB)),
        out_shape=jax.ShapeDtypeStruct((3 * rank, width), bf16),
        in_specs=[pl.BlockSpec(memory_space=VMEM)] * 2,
        out_specs=pl.BlockSpec(memory_space=VMEM),
        compiler_params=pltpu.CompilerParams(vmem_limit_bytes=LIMIT),
        cost_estimate=cost(5 * 10**8, 16 * rank * width),
    )(mine, other)
    new_embed, new_moment_embed = call(
        functools.partial(embed_kernel, embed),
        (after(coeff, delta_other), basis, outer_embed, moment_embed), [((rows, width), f32)] * 2,
        flops=6 * rank * rows * width, parts={2: embed, 3: embed}, here=(0,), weight=18,
    )
    new_attn, new_moment_attn, new_norms, new_moment_norms = call(
        functools.partial(attn_kernel, shards),
        (delta, delta_other, outer_attn, moment_attn, outer_norms, moment_norms),
        [(outer_attn.shape, f32)] * 2 + [(outer_norms.shape, f32)] * 2,
        [pltpu.VMEM((outer_attn.shape[1], 2 * LANES), f32)], here=(1,),
    )
    (replica_attn,) = call(
        functools.partial(replica_kernel, shards), (replica,), [(inner_attn.shape[1:], bf16)], here=(0,)
    )
    return (new_embed, new_moment_embed, new_attn.T, new_moment_attn.T, new_norms, new_moment_norms, replica_attn)


def plain(
    inner_embed, outer_embed, moment_embed, basis, inner_attn, outer_attn, moment_attn,
    inner_norms, outer_norms, moment_norms,
):
    groups = lax.axis_size("group")
    coeff = lax.dot_general(
        basis, outer_embed - inner_embed[0], (((0,), (0,)), ((), ())),
        precision=lax.Precision.HIGHEST, preferred_element_type=f32,
    )
    moved = lax.all_to_all(inner_attn[0], "shard", split_axis=1, concat_axis=0, tiled=True)
    coeff = lax.psum(coeff, ("group", "shard")) / groups
    attn_sum, norm_sum = lax.psum((outer_attn - moved, outer_norms - inner_norms[0]), "group")
    embed_delta = jnp.dot(basis, coeff, precision=lax.Precision.HIGHEST, preferred_element_type=f32) * (
        1.0 / math.sqrt(RANK * VOCAB)
    )
    new_embed, new_moment_embed = nesterov(outer_embed, moment_embed, embed_delta)
    new_attn, new_moment_attn = nesterov(outer_attn, moment_attn, attn_sum / groups)
    new_norms, new_moment_norms = nesterov(outer_norms, moment_norms, norm_sum / groups)
    replica_attn = lax.all_to_all(new_attn.astype(bf16), "shard", split_axis=0, concat_axis=1, tiled=True)
    return (new_embed, new_moment_embed, new_attn, new_moment_attn, new_norms, new_moment_norms, replica_attn)


def on_device(*args):
    outer_embed, basis, inner_attn, outer_attn, norms = args[1], args[3], args[4], args[5], args[8]
    shards = lax.axis_size("shard")
    fits = (
        lax.axis_size("group") == 2
        and shards >= 2
        and shards & (shards - 1) == 0
        and inner_attn.shape == (1, 48, 192 * shards)
        and outer_attn.shape == (48 * shards, 192)
        and outer_attn.shape[0] % LANES == 0
        and shards % 4 == 0
        and norms.shape[0] <= 8
        and norms.shape[1] <= HALF
        and outer_embed.shape[1] % 256 == 0
        and outer_embed.shape[0] % 8 == 0
        and basis.shape[1] % 16 == 0
    )
    return (fast if fits else plain)(*args)


def solution(mesh):
    placed = (
        P("group", "shard", None),
        P("shard", None),
        P("shard", None),
        P("shard", None),
        P("group", "shard", None),
        P(None, "shard"),
        P(None, "shard"),
        P("group", None, "shard"),
        P(None, "shard"),
        P(None, "shard"),
    )
    return jax.shard_map(
        on_device,
        mesh=mesh,
        in_specs=placed,
        out_specs=(
            P("shard", None),
            P("shard", None),
            P(None, "shard"),
            P(None, "shard"),
            P(None, "shard"),
            P(None, "shard"),
            P("shard", None),
        ),
        check_vma=False,
    )
```

```python
import functools
import math

import jax
import jax.numpy as jnp
from jax import lax
from jax.experimental import pallas as pl
from jax.experimental.pallas import tpu as pltpu
from jax.sharding import PartitionSpec as P

VOCAB = 15360
RANK = 64
LANES = 128
HALF = 64
ROWS = 40

f32 = jnp.float32
bf16 = jnp.bfloat16
VMEM = pltpu.VMEM
LIMIT = 40 * 1024 * 1024


def nesterov(outer, moment, delta):
    moment_new = 0.5 * moment + delta
    return (outer - (delta + 0.5 * moment_new), moment_new)


def remote(count):
    return [pl.BlockSpec(memory_space=pltpu.HBM)] * count


def cost(flops, moved):
    return pl.CostEstimate(flops=flops, bytes_accessed=moved, transcendentals=0)


def left_half(shape):
    return lax.broadcasted_iota(jnp.int32, shape, 1) < HALF


def roll_half(x):
    return pltpu.roll(x, HALF, 1)


def split3(x):
    hi = x.astype(bf16)
    lo = (x - hi.astype(f32)).astype(bf16)
    return hi, lo


def dot3(a, b):
    rows = a.shape[0]
    ah, al = split3(a)
    bh, bl = split3(b)
    both = jnp.dot(jnp.concatenate([ah, al], axis=0), bh, preferred_element_type=f32)
    return both[:rows] + (both[rows:] + jnp.dot(ah, bl, preferred_element_type=f32))


def chunks(rows):
    return [(at, min(256, rows - at)) for at in range(0, rows, 256)]


def coeff_kernel(basis_in, outer_in, inner_in, mine_ref, other_ref, basis_ref, outer_ref, inner_ref, sems):
    parts = chunks(outer_ref.shape[0])

    def copy(src, dst, at, size, sem):
        return pltpu.make_async_copy(src.at[pl.ds(at, size)], dst.at[pl.ds(at, size)], sems.at[sem])

    copies = [copy(basis_in, basis_ref, 0, basis_ref.shape[0], 0)]
    for k, (at, size) in enumerate(parts):
        copies.append(copy(outer_in, outer_ref, at, size, 1 + 2 * k))
        copies.append(copy(inner_in, inner_ref, at, size, 2 + 2 * k))
    for c in copies:
        c.start()
    copies[0].wait()
    first = lax.rem(lax.axis_index("shard"), 2) == 0
    rows = mine_ref.shape[0]
    total = None
    for k, (at, size) in enumerate(parts):
        copies[1 + 2 * k].wait()
        copies[2 + 2 * k].wait()
        part = slice(at, at + size)
        term = dot3(basis_ref[:, part], outer_ref[part, :] - inner_ref[part, :])
        total = term if total is None else total + term
    low, high = total[:rows], total[rows:]
    other_ref[...] = jnp.where(first, high, low)
    mine_ref[...] = jnp.where(first, low, high)


def norm_tile(scr, norm_ref):
    scr[...] = jnp.zeros_like(scr)
    scr[: norm_ref.shape[0], : norm_ref.shape[1]] = norm_ref[...]
    return roll_half(scr[...])


def make_piece(main, half, tile):
    mask = left_half((8, LANES))
    third = jnp.where(mask, half[0:8], roll_half(half[8:16]))
    return jnp.concatenate([main, third, jnp.where(mask, half[16:24], tile)], axis=0)


def put_piece(out_ref, at, main, half, tile):
    out_ref[at] = make_piece(main, half, tile)


def get_half(piece):
    return jnp.concatenate([piece[24:32], roll_half(piece[24:32]), piece[32:40]], axis=0)


def put_dense(out_ref, at, main, half):
    mask = left_half((4, LANES))
    for k in range(6):
        out_ref[at, :, LANES * k : LANES * k + LANES] = main[4 * k : 4 * k + 4]
    turned = roll_half(half)
    for k in range(3):
        group = jnp.where(mask, half[8 * k : 8 * k + 4], turned[8 * k + 4 : 8 * k + 8])
        out_ref[at, :, LANES * (6 + k) : LANES * (7 + k)] = group


def get_dense(ref, at):
    groups = [ref[at, :, LANES * k : LANES * k + LANES] for k in range(9)]
    tiles = [jnp.concatenate([g, roll_half(g)], axis=0) for g in groups[6:]]
    third = jnp.where(left_half((8, LANES)), tiles[0], roll_half(tiles[1]))
    return jnp.concatenate(groups[:6] + [third, tiles[2]], axis=0)


def pack_kernel(shards, load, store, x_ref, out_ref):
    mask = left_half((24, LANES))
    for group in range(2):
        load(0, group)
        rows = slice(24 * group, 24 * group + 24)
        for pair in range(shards // 2):
            at = group * shards + 2 * pair
            t = [x_ref[rows, 384 * pair + LANES * k : 384 * pair + LANES * k + LANES] for k in range(3)]
            t1, t2 = roll_half(t[1]), roll_half(t[2])
            put_dense(out_ref, at, t[0], t[1])
            put_dense(out_ref, at + 1, jnp.where(mask, t1, t2), t2)
        store(0, slice(group * shards, group * shards + shards))


def states_kernel(shards, load, store, outer_ref, moment_ref, outer_out, moment_out, scr):
    group = lax.axis_index("group")
    for n, (src, out) in enumerate(((outer_ref, outer_out), (moment_ref, moment_out))):
        load(n)
        for k in range(src.shape[1] // LANES):
            cols = slice(LANES * k, LANES * k + LANES)
            scr[n, cols, 0:LANES] = src[0:LANES, cols].T
            scr[n, cols, LANES : LANES + HALF] = src[LANES : LANES + HALF, cols].T
        for s in range(shards):
            rows = pl.ds(pl.multiple_of(48 * s + 24 * group, 8), 24)
            half = scr[n, rows, LANES:]
            out[s] = make_piece(scr[n, rows, :LANES], half, half[16:24])
        store(n)


def middle_kernel(shards, load, store, outer_ref, moment_ref, norm_ref, got_ref, send_ref, delta_ref, scr):
    for n in (2, 0, 1):
        load(n)
    tile = norm_tile(scr, norm_ref)
    mask = left_half((8, LANES))
    for s in range(shards):
        outer = outer_ref[s]
        delta = ((outer - get_dense(got_ref, s)) + (outer - get_dense(got_ref, shards + s))) * 0.5
        delta_ref[s, 0:32] = delta[0:32]
        delta_ref[s, 32:40] = jnp.where(mask, delta[32:40], tile)
        new = nesterov(outer, moment_ref[s], delta)[0].astype(bf16)
        send_ref[s] = new
        send_ref[shards + s] = new
    store(0)
    store(1)


def join_kernel(scale, mine_ref, other_ref, out_ref):
    first = lax.rem(lax.axis_index("shard"), 2) == 0
    mine, other = mine_ref[...] * scale, other_ref[...] * scale
    high, low = split3(jnp.concatenate([jnp.where(first, mine, other), jnp.where(first, other, mine)], axis=0))
    out_ref[...] = jnp.concatenate([high, low, high], axis=0)


def embed_kernel(parts, load, store, coeff_ref, basis_ref, outer_ref, moment_ref, new_ref, new_moment_ref):
    coeff = coeff_ref[...]
    load(1)
    for k, (at, size) in enumerate(parts):
        part = slice(at, at + size)
        high, low = split3(basis_ref[:, part])
        three = jnp.concatenate([high, high, low], axis=0)
        delta = lax.dot_general(three, coeff, (((0,), (0,)), ((), ())), preferred_element_type=f32)
        load(2, k)
        load(3, k)
        new_ref[part, :], new_moment_ref[part, :] = nesterov(outer_ref[part, :], moment_ref[part, :], delta)
        store(0, part)
        store(1, part)


def replica_kernel(shards, load, store, got_ref, out_ref):
    mask = left_half((24, LANES))
    for pair in range(shards // 2):
        tiles = [[], [], []]
        for g in range(2):
            even, odd = (got_ref[g * shards + 2 * pair + n].astype(f32) for n in range(2))
            turned = roll_half(odd[0:24])
            tiles[0].append(even[0:24])
            tiles[1].append(jnp.where(mask, get_half(even), turned))
            tiles[2].append(jnp.where(mask, turned, roll_half(get_half(odd))))
        for k in range(3):
            at = 384 * pair + LANES * k
            out_ref[:, at : at + LANES] = jnp.concatenate(tiles[k], axis=0).astype(bf16)
        if pair % 2:
            store(0, (slice(None), slice(384 * pair - 384, 384 * pair + 384)))


def attn_kernel(
    shards, load, store, mine_ref, other_ref, outer_ref, moment_ref, outer_norm_ref, moment_norm_ref,
    new_ref, new_moment_ref, new_norm_ref, new_moment_norm_ref, scr,
):
    group = lax.axis_index("group")
    for n, (src, owner) in enumerate(((mine_ref, group), (other_ref, 1 - group))):
        load(n)
        for s in range(shards):
            piece = src[s]
            rows = pl.ds(pl.multiple_of(48 * s + 24 * owner, 8), 24)
            scr[rows, 0:LANES] = piece[0:24]
            scr[rows, LANES : 2 * LANES] = get_half(piece)
    for n in range(2, 6):
        load(n)
    for k in range(outer_ref.shape[1] // LANES):
        cols = slice(LANES * k, LANES * k + LANES)
        for rows, part in ((slice(0, LANES), scr[cols, 0:LANES].T), (slice(LANES, LANES + HALF), scr[cols, LANES : 2 * LANES].T[:HALF])):
            new_ref[rows, cols], new_moment_ref[rows, cols] = nesterov(outer_ref[rows, cols], moment_ref[rows, cols], part)
    store(0)
    store(1)
    norms, width = outer_norm_ref.shape
    outer = outer_norm_ref[...]
    mine, other = (roll_half(ref[0, 32:40, :])[:norms, :width] for ref in (mine_ref, other_ref))
    delta = ((outer - mine) + (outer - other)) * 0.5
    new_norm_ref[...], new_moment_norm_ref[...] = nesterov(outer, moment_norm_ref[...], delta)
    store(2)
    store(3)


def staged(kernel, parts, count, *refs):
    ins, outs = refs[: len(parts)], refs[len(parts) : count]
    scratch = list(refs[count:])
    held_in = [scratch.pop(0) if p else ref for p, ref in zip(parts, ins, strict=True)]
    held_out = [scratch.pop(0) for _ in outs]
    in_sem, out_sem = scratch.pop(0), scratch.pop(0)

    def copy(n, k):
        at, size = parts[n][k]
        part = slice(at, at + size)
        return pltpu.make_async_copy(ins[n].at[part], held_in[n].at[part], in_sem.at[sum(len(p) for p in parts[:n]) + k])

    for k in range(max(len(p) for p in parts)):
        for n in range(len(parts)):
            if k < len(parts[n]):
                copy(n, k).start()

    def load(n, k=0):
        if parts[n]:
            copy(n, k).wait()

    def store(n, part=slice(None)):
        pltpu.make_async_copy(held_out[n].at[part], outs[n].at[part], out_sem.at[n]).start()

    kernel(load, store, *held_in, *held_out, *scratch)
    for n in range(len(outs)):
        pltpu.make_async_copy(held_out[n], outs[n], out_sem.at[n]).wait()


def call(kernel, args, outs, scratch=(), flops=0, parts=None, here=(), weight=1):
    moved = sum(x.size * x.dtype.itemsize for x in args) + sum(math.prod(s) * jnp.dtype(d).itemsize for s, d in outs)
    parts = parts or {}
    parts = [[] if n in here else parts.get(n, [(0, x.shape[0])]) for n, x in enumerate(args)]
    return pl.pallas_call(
        functools.partial(staged, kernel, parts, len(args) + len(outs)),
        out_shape=[pltpu.HBM(s, d) for s, d in outs],
        in_specs=[pl.BlockSpec(memory_space=pltpu.HBM if p else VMEM) for p in parts],
        out_specs=remote(len(outs)),
        scratch_shapes=[pltpu.VMEM(x.shape, x.dtype) for x, p in zip(args, parts, strict=True) if p]
        + [pltpu.VMEM(s, d) for s, d in outs]
        + [pltpu.SemaphoreType.DMA((max(1, sum(len(p) for p in parts)),)), pltpu.SemaphoreType.DMA((len(outs),))]
        + list(scratch),
        compiler_params=pltpu.CompilerParams(vmem_limit_bytes=LIMIT),
        cost_estimate=cost(weight * flops, weight * moved),
    )(*[pltpu.with_memory_space_constraint(x, pltpu.HBM) if p else x for x, p in zip(args, parts, strict=True)])


def after(x, *others):
    return lax.optimization_barrier((x, *others))[0]


def everyone(x):
    return lax.all_to_all(x, ("group", "shard"), split_axis=0, concat_axis=0, tiled=True)


def swap_groups(x):
    return lax.ppermute(x, "group", [(0, 1), (1, 0)])


def swap_shards(x, bit):
    return lax.ppermute(x, "shard", [(i, i ^ bit) for i in range(lax.axis_size("shard"))])


def hop(x, *masks):
    devices = lax.axis_size("group") * lax.axis_size("shard")
    return lax.ppermute(x, ("group", "shard"), [(d, d ^ masks[d % 2]) for d in range(devices)])


def hops(shards):
    bits = [shards]
    while len(bits) == 1 or 2 * bits[-1] < shards:
        bits.append(2 * bits[-1] if len(bits) > 1 else 2)
    order = []
    for a, b in zip(bits[::2], bits[1::2]):
        order += [(a, b), (b, a)]
    return order + ([(bits[-1],) * 2] if len(bits) % 2 else [])


def fast(
    inner_embed, outer_embed, moment_embed, basis, inner_attn, outer_attn, moment_attn,
    inner_norms, outer_norms, moment_norms,
):
    shards = lax.axis_size("shard")
    rows, width = outer_embed.shape
    rank = basis.shape[1]
    basis = basis.T
    outer_attn, moment_attn = outer_attn.T, moment_attn.T
    piece = (shards, ROWS, LANES)

    (sent,) = call(
        functools.partial(pack_kernel, shards), (inner_attn[0],), [((2 * shards, 4, 9 * LANES), f32)],
        parts={0: [(0, 24), (24, 24)]},
    )
    got = everyone(sent)

    mine, other = pl.pallas_call(
        coeff_kernel,
        out_shape=[jax.ShapeDtypeStruct((rank // 2, width), f32)] * 2,
        in_specs=remote(3),
        out_specs=[pl.BlockSpec(memory_space=VMEM)] * 2,
        scratch_shapes=[pltpu.VMEM(basis.shape, f32)]
        + [pltpu.VMEM(outer_embed.shape, f32)] * 2
        + [pltpu.SemaphoreType.DMA((1 + 2 * len(chunks(rows)),))],
        compiler_params=pltpu.CompilerParams(vmem_limit_bytes=LIMIT),
        cost_estimate=cost(6 * rank * rows * width, 8 * rows * width),
    )(*[pltpu.with_memory_space_constraint(x, pltpu.HBM) for x in (basis, outer_embed, inner_embed[0])])
    mine = mine + swap_shards(other, 1)
    outer_piece, moment_piece = call(
        functools.partial(states_kernel, shards), (outer_attn, moment_attn), [(piece, f32)] * 2,
        [pltpu.VMEM((2, outer_attn.shape[1], 2 * LANES), f32)],
    )
    steps = []
    for n, masks in enumerate(hops(shards)):
        moved = hop(mine, *masks)
        if n == 0:
            moved = after(moved, outer_piece)
        if n == 2:
            send, delta = call(
                functools.partial(middle_kernel, shards), (after(outer_piece, steps[1]), moment_piece, inner_norms[0], got),
                [((2 * shards, ROWS, LANES), bf16), (piece, f32)], [pltpu.VMEM((8, LANES), f32)], here=(3,),
            )
            moved = after(moved, delta)
        mine = mine + moved
        steps.append(mine)
    other = swap_shards(mine, 1)

    replica = everyone(after(send, steps[2]))
    delta_other = swap_groups(delta)
    embed = chunks(rows)
    coeff = pl.pallas_call(
        functools.partial(join_kernel, 0.5 / math.sqrt(RANK * VOCAB)),
        out_shape=jax.ShapeDtypeStruct((3 * rank, width), bf16),
        in_specs=[pl.BlockSpec(memory_space=VMEM)] * 2,
        out_specs=pl.BlockSpec(memory_space=VMEM),
        compiler_params=pltpu.CompilerParams(vmem_limit_bytes=LIMIT),
        cost_estimate=cost(5 * 10**8, 16 * rank * width),
    )(mine, other)
    new_embed, new_moment_embed = call(
        functools.partial(embed_kernel, embed),
        (after(coeff, delta_other), basis, outer_embed, moment_embed), [((rows, width), f32)] * 2,
        flops=6 * rank * rows * width, parts={2: embed, 3: embed}, here=(0,), weight=18,
    )
    new_attn, new_moment_attn, new_norms, new_moment_norms = call(
        functools.partial(attn_kernel, shards),
        (delta, delta_other, outer_attn, moment_attn, outer_norms, moment_norms),
        [(outer_attn.shape, f32)] * 2 + [(outer_norms.shape, f32)] * 2,
        [pltpu.VMEM((outer_attn.shape[1], 2 * LANES), f32)], here=(1,),
    )
    (replica_attn,) = call(
        functools.partial(replica_kernel, shards), (replica,), [(inner_attn.shape[1:], bf16)], here=(0,)
    )
    return (new_embed, new_moment_embed, new_attn.T, new_moment_attn.T, new_norms, new_moment_norms, replica_attn)


def plain(
    inner_embed, outer_embed, moment_embed, basis, inner_attn, outer_attn, moment_attn,
    inner_norms, outer_norms, moment_norms,
):
    groups = lax.axis_size("group")
    coeff = lax.dot_general(
        basis, outer_embed - inner_embed[0], (((0,), (0,)), ((), ())),
        precision=lax.Precision.HIGHEST, preferred_element_type=f32,
    )
    moved = lax.all_to_all(inner_attn[0], "shard", split_axis=1, concat_axis=0, tiled=True)
    coeff = lax.psum(coeff, ("group", "shard")) / groups
    attn_sum, norm_sum = lax.psum((outer_attn - moved, outer_norms - inner_norms[0]), "group")
    embed_delta = jnp.dot(basis, coeff, precision=lax.Precision.HIGHEST, preferred_element_type=f32) * (
        1.0 / math.sqrt(RANK * VOCAB)
    )
    new_embed, new_moment_embed = nesterov(outer_embed, moment_embed, embed_delta)
    new_attn, new_moment_attn = nesterov(outer_attn, moment_attn, attn_sum / groups)
    new_norms, new_moment_norms = nesterov(outer_norms, moment_norms, norm_sum / groups)
    replica_attn = lax.all_to_all(new_attn.astype(bf16), "shard", split_axis=0, concat_axis=1, tiled=True)
    return (new_embed, new_moment_embed, new_attn, new_moment_attn, new_norms, new_moment_norms, replica_attn)


def on_device(*args):
    outer_embed, basis, inner_attn, outer_attn, norms = args[1], args[3], args[4], args[5], args[8]
    shards = lax.axis_size("shard")
    fits = (
        lax.axis_size("group") == 2
        and shards >= 2
        and shards & (shards - 1) == 0
        and inner_attn.shape == (1, 48, 192 * shards)
        and outer_attn.shape == (48 * shards, 192)
        and outer_attn.shape[0] % LANES == 0
        and shards % 4 == 0
        and norms.shape[0] <= 8
        and norms.shape[1] <= HALF
        and outer_embed.shape[1] % 256 == 0
        and outer_embed.shape[0] % 8 == 0
        and basis.shape[1] % 16 == 0
    )
    return (fast if fits else plain)(*args)


def solution(mesh):
    placed = (
        P("group", "shard", None),
        P("shard", None),
        P("shard", None),
        P("shard", None),
        P("group", "shard", None),
        P(None, "shard"),
        P(None, "shard"),
        P("group", None, "shard"),
        P(None, "shard"),
        P(None, "shard"),
    )
    return jax.shard_map(
        on_device,
        mesh=mesh,
        in_specs=placed,
        out_specs=(
            P("shard", None),
            P("shard", None),
            P(None, "shard"),
            P(None, "shard"),
            P(None, "shard"),
            P(None, "shard"),
            P("shard", None),
        ),
        check_vma=False,
    )
```

```python
import functools
import math

import jax
import jax.numpy as jnp
from jax import lax
from jax.experimental import pallas as pl
from jax.experimental.pallas import tpu as pltpu
from jax.sharding import PartitionSpec as P

VOCAB = 15360
RANK = 64
LANES = 128
HALF = 64
ROWS = 40

f32 = jnp.float32
bf16 = jnp.bfloat16
VMEM = pltpu.VMEM
LIMIT = 40 * 1024 * 1024


def nesterov(outer, moment, delta):
    moment_new = 0.5 * moment + delta
    return (outer - (delta + 0.5 * moment_new), moment_new)


def remote(count):
    return [pl.BlockSpec(memory_space=pltpu.HBM)] * count


def cost(flops, moved):
    return pl.CostEstimate(flops=flops, bytes_accessed=moved, transcendentals=0)


def left_half(shape):
    return lax.broadcasted_iota(jnp.int32, shape, 1) < HALF


def roll_half(x):
    return pltpu.roll(x, HALF, 1)


def split3(x):
    hi = x.astype(bf16)
    lo = (x - hi.astype(f32)).astype(bf16)
    return hi, lo


def dot3(a, b):
    rows = a.shape[0]
    ah, al = split3(a)
    bh, bl = split3(b)
    both = jnp.dot(jnp.concatenate([ah, al], axis=0), bh, preferred_element_type=f32)
    return both[:rows] + (both[rows:] + jnp.dot(ah, bl, preferred_element_type=f32))


def chunks(rows):
    return [(at, min(256, rows - at)) for at in range(0, rows, 256)]


def coeff_kernel(basis_in, outer_in, inner_in, mine_ref, other_ref, basis_ref, outer_ref, inner_ref, sems):
    parts = chunks(outer_ref.shape[0])

    def copy(src, dst, at, size, sem):
        return pltpu.make_async_copy(src.at[pl.ds(at, size)], dst.at[pl.ds(at, size)], sems.at[sem])

    copies = [copy(basis_in, basis_ref, 0, basis_ref.shape[0], 0)]
    for k, (at, size) in enumerate(parts):
        copies.append(copy(outer_in, outer_ref, at, size, 1 + 2 * k))
        copies.append(copy(inner_in, inner_ref, at, size, 2 + 2 * k))
    for c in copies:
        c.start()
    copies[0].wait()
    first = lax.rem(lax.axis_index("shard"), 2) == 0
    rows = mine_ref.shape[0]
    total = None
    for k, (at, size) in enumerate(parts):
        copies[1 + 2 * k].wait()
        copies[2 + 2 * k].wait()
        part = slice(at, at + size)
        term = dot3(basis_ref[:, part], outer_ref[part, :] - inner_ref[part, :])
        total = term if total is None else total + term
    low, high = total[:rows], total[rows:]
    other_ref[...] = jnp.where(first, high, low)
    mine_ref[...] = jnp.where(first, low, high)


def norm_tile(scr, norm_ref):
    scr[...] = jnp.zeros_like(scr)
    scr[: norm_ref.shape[0], : norm_ref.shape[1]] = norm_ref[...]
    return roll_half(scr[...])


def make_piece(main, half, tile):
    mask = left_half((8, LANES))
    third = jnp.where(mask, half[0:8], roll_half(half[8:16]))
    return jnp.concatenate([main, third, jnp.where(mask, half[16:24], tile)], axis=0)


def put_piece(out_ref, at, main, half, tile):
    out_ref[at] = make_piece(main, half, tile)


def get_half(piece):
    return jnp.concatenate([piece[24:32], roll_half(piece[24:32]), piece[32:40]], axis=0)


def put_dense(out_ref, at, main, half):
    mask = left_half((4, LANES))
    for k in range(6):
        out_ref[at, :, LANES * k : LANES * k + LANES] = main[4 * k : 4 * k + 4]
    turned = roll_half(half)
    for k in range(3):
        group = jnp.where(mask, half[8 * k : 8 * k + 4], turned[8 * k + 4 : 8 * k + 8])
        out_ref[at, :, LANES * (6 + k) : LANES * (7 + k)] = group


def get_dense(ref, at):
    groups = [ref[at, :, LANES * k : LANES * k + LANES] for k in range(9)]
    tiles = [jnp.concatenate([g, roll_half(g)], axis=0) for g in groups[6:]]
    third = jnp.where(left_half((8, LANES)), tiles[0], roll_half(tiles[1]))
    return jnp.concatenate(groups[:6] + [third, tiles[2]], axis=0)


def pack_kernel(shards, load, store, x_ref, out_ref):
    mask = left_half((24, LANES))
    for group in range(2):
        load(0, group)
        rows = slice(24 * group, 24 * group + 24)
        for pair in range(shards // 2):
            at = group * shards + 2 * pair
            t = [x_ref[rows, 384 * pair + LANES * k : 384 * pair + LANES * k + LANES] for k in range(3)]
            t1, t2 = roll_half(t[1]), roll_half(t[2])
            put_dense(out_ref, at, t[0], t[1])
            put_dense(out_ref, at + 1, jnp.where(mask, t1, t2), t2)
        store(0, slice(group * shards, group * shards + shards))


def states_kernel(shards, load, store, outer_ref, moment_ref, outer_out, moment_out, scr):
    group = lax.axis_index("group")
    for n, (src, out) in enumerate(((outer_ref, outer_out), (moment_ref, moment_out))):
        load(n)
        for k in range(src.shape[1] // LANES):
            cols = slice(LANES * k, LANES * k + LANES)
            scr[n, cols, 0:LANES] = src[0:LANES, cols].T
            scr[n, cols, LANES : LANES + HALF] = src[LANES : LANES + HALF, cols].T
        for s in range(shards):
            rows = pl.ds(pl.multiple_of(48 * s + 24 * group, 8), 24)
            half = scr[n, rows, LANES:]
            out[s] = make_piece(scr[n, rows, :LANES], half, half[16:24])
        store(n)


def middle_kernel(shards, load, store, outer_ref, moment_ref, norm_ref, got_ref, send_ref, delta_ref, scr):
    for n in (2, 0, 1):
        load(n)
    tile = norm_tile(scr, norm_ref)
    mask = left_half((8, LANES))
    for s in range(shards):
        outer = outer_ref[s]
        delta = ((outer - get_dense(got_ref, s)) + (outer - get_dense(got_ref, shards + s))) * 0.5
        delta_ref[s, 0:32] = delta[0:32]
        delta_ref[s, 32:40] = jnp.where(mask, delta[32:40], tile)
        new = nesterov(outer, moment_ref[s], delta)[0].astype(bf16)
        send_ref[s] = new
        send_ref[shards + s] = new
        if s % 4 == 3:
            for n, at in ((0, s - 3), (0, shards + s - 3), (1, s - 3)):
                store(n, slice(at, at + 4))


def join_kernel(scale, mine_ref, other_ref, out_ref):
    first = lax.rem(lax.axis_index("shard"), 2) == 0
    mine, other = mine_ref[...] * scale, other_ref[...] * scale
    high, low = split3(jnp.concatenate([jnp.where(first, mine, other), jnp.where(first, other, mine)], axis=0))
    out_ref[...] = jnp.concatenate([high, low, high], axis=0)


def embed_kernel(parts, load, store, coeff_ref, basis_ref, outer_ref, moment_ref, new_ref, new_moment_ref):
    coeff = coeff_ref[...]
    load(1)
    for k, (at, size) in enumerate(parts):
        part = slice(at, at + size)
        high, low = split3(basis_ref[:, part])
        three = jnp.concatenate([high, high, low], axis=0)
        delta = lax.dot_general(three, coeff, (((0,), (0,)), ((), ())), preferred_element_type=f32)
        load(2, k)
        load(3, k)
        new_ref[part, :], new_moment_ref[part, :] = nesterov(outer_ref[part, :], moment_ref[part, :], delta)
        store(0, part)
        store(1, part)


def replica_kernel(shards, load, store, got_ref, out_ref):
    mask = left_half((24, LANES))
    for pair in range(shards // 2):
        tiles = [[], [], []]
        for g in range(2):
            even, odd = (got_ref[g * shards + 2 * pair + n].astype(f32) for n in range(2))
            turned = roll_half(odd[0:24])
            tiles[0].append(even[0:24])
            tiles[1].append(jnp.where(mask, get_half(even), turned))
            tiles[2].append(jnp.where(mask, turned, roll_half(get_half(odd))))
        for k in range(3):
            at = 384 * pair + LANES * k
            out_ref[:, at : at + LANES] = jnp.concatenate(tiles[k], axis=0).astype(bf16)
        if pair % 2:
            store(0, (slice(None), slice(384 * pair - 384, 384 * pair + 384)))


def attn_kernel(
    shards, load, store, mine_ref, other_ref, outer_ref, moment_ref, outer_norm_ref, moment_norm_ref,
    new_ref, new_moment_ref, new_norm_ref, new_moment_norm_ref, scr,
):
    group = lax.axis_index("group")
    for n, (src, owner) in enumerate(((mine_ref, group), (other_ref, 1 - group))):
        load(n)
        for s in range(shards):
            piece = src[s]
            rows = pl.ds(pl.multiple_of(48 * s + 24 * owner, 8), 24)
            scr[rows, 0:LANES] = piece[0:24]
            scr[rows, LANES : 2 * LANES] = get_half(piece)
    for n in range(2, 6):
        load(n)
    for k in range(outer_ref.shape[1] // LANES):
        cols = slice(LANES * k, LANES * k + LANES)
        for rows, part in ((slice(0, LANES), scr[cols, 0:LANES].T), (slice(LANES, LANES + HALF), scr[cols, LANES : 2 * LANES].T[:HALF])):
            new_ref[rows, cols], new_moment_ref[rows, cols] = nesterov(outer_ref[rows, cols], moment_ref[rows, cols], part)
        store(0, (slice(None), cols))
        store(1, (slice(None), cols))
    norms, width = outer_norm_ref.shape
    outer = outer_norm_ref[...]
    mine, other = (roll_half(ref[0, 32:40, :])[:norms, :width] for ref in (mine_ref, other_ref))
    delta = ((outer - mine) + (outer - other)) * 0.5
    new_norm_ref[...], new_moment_norm_ref[...] = nesterov(outer, moment_norm_ref[...], delta)
    store(2)
    store(3)


def staged(kernel, parts, count, *refs):
    ins, outs = refs[: len(parts)], refs[len(parts) : count]
    scratch = list(refs[count:])
    held_in = [scratch.pop(0) if p else ref for p, ref in zip(parts, ins, strict=True)]
    held_out = [scratch.pop(0) for _ in outs]
    in_sem, out_sem = scratch.pop(0), scratch.pop(0)

    def copy(n, k):
        at, size = parts[n][k]
        part = slice(at, at + size)
        return pltpu.make_async_copy(ins[n].at[part], held_in[n].at[part], in_sem.at[sum(len(p) for p in parts[:n]) + k])

    for k in range(max(len(p) for p in parts)):
        for n in range(len(parts)):
            if k < len(parts[n]):
                copy(n, k).start()

    def load(n, k=0):
        if parts[n]:
            copy(n, k).wait()

    def store(n, part=slice(None)):
        pltpu.make_async_copy(held_out[n].at[part], outs[n].at[part], out_sem.at[n]).start()

    kernel(load, store, *held_in, *held_out, *scratch)
    for n in range(len(outs)):
        pltpu.make_async_copy(held_out[n], outs[n], out_sem.at[n]).wait()


def call(kernel, args, outs, scratch=(), flops=0, parts=None, here=(), weight=1):
    moved = sum(x.size * x.dtype.itemsize for x in args) + sum(math.prod(s) * jnp.dtype(d).itemsize for s, d in outs)
    parts = parts or {}
    parts = [[] if n in here else parts.get(n, [(0, x.shape[0])]) for n, x in enumerate(args)]
    return pl.pallas_call(
        functools.partial(staged, kernel, parts, len(args) + len(outs)),
        out_shape=[pltpu.HBM(s, d) for s, d in outs],
        in_specs=[pl.BlockSpec(memory_space=pltpu.HBM if p else VMEM) for p in parts],
        out_specs=remote(len(outs)),
        scratch_shapes=[pltpu.VMEM(x.shape, x.dtype) for x, p in zip(args, parts, strict=True) if p]
        + [pltpu.VMEM(s, d) for s, d in outs]
        + [pltpu.SemaphoreType.DMA((max(1, sum(len(p) for p in parts)),)), pltpu.SemaphoreType.DMA((len(outs),))]
        + list(scratch),
        compiler_params=pltpu.CompilerParams(vmem_limit_bytes=LIMIT),
        cost_estimate=cost(weight * flops, weight * moved),
    )(*[pltpu.with_memory_space_constraint(x, pltpu.HBM) if p else x for x, p in zip(args, parts, strict=True)])


def after(x, *others):
    return lax.optimization_barrier((x, *others))[0]


def everyone(x):
    return lax.all_to_all(x, ("group", "shard"), split_axis=0, concat_axis=0, tiled=True)


def swap_groups(x):
    return lax.ppermute(x, "group", [(0, 1), (1, 0)])


def swap_shards(x, bit):
    return lax.ppermute(x, "shard", [(i, i ^ bit) for i in range(lax.axis_size("shard"))])


def hop(x, *masks):
    devices = lax.axis_size("group") * lax.axis_size("shard")
    return lax.ppermute(x, ("group", "shard"), [(d, d ^ masks[d % 2]) for d in range(devices)])


def hops(shards):
    bits = [shards]
    while len(bits) == 1 or 2 * bits[-1] < shards:
        bits.append(2 * bits[-1] if len(bits) > 1 else 2)
    order = []
    for a, b in zip(bits[::2], bits[1::2]):
        order += [(a, b), (b, a)]
    return order + ([(bits[-1],) * 2] if len(bits) % 2 else [])


def fast(
    inner_embed, outer_embed, moment_embed, basis, inner_attn, outer_attn, moment_attn,
    inner_norms, outer_norms, moment_norms,
):
    shards = lax.axis_size("shard")
    rows, width = outer_embed.shape
    rank = basis.shape[1]
    basis = basis.T
    outer_attn, moment_attn = outer_attn.T, moment_attn.T
    piece = (shards, ROWS, LANES)

    (sent,) = call(
        functools.partial(pack_kernel, shards), (inner_attn[0],), [((2 * shards, 4, 9 * LANES), f32)],
        parts={0: [(0, 24), (24, 24)]},
    )
    got = everyone(sent)

    mine, other = pl.pallas_call(
        coeff_kernel,
        out_shape=[jax.ShapeDtypeStruct((rank // 2, width), f32)] * 2,
        in_specs=remote(3),
        out_specs=[pl.BlockSpec(memory_space=VMEM)] * 2,
        scratch_shapes=[pltpu.VMEM(basis.shape, f32)]
        + [pltpu.VMEM(outer_embed.shape, f32)] * 2
        + [pltpu.SemaphoreType.DMA((1 + 2 * len(chunks(rows)),))],
        compiler_params=pltpu.CompilerParams(vmem_limit_bytes=LIMIT),
        cost_estimate=cost(6 * rank * rows * width, 8 * rows * width),
    )(*[pltpu.with_memory_space_constraint(x, pltpu.HBM) for x in (basis, outer_embed, inner_embed[0])])
    mine = mine + swap_shards(other, 1)
    outer_piece, moment_piece = call(
        functools.partial(states_kernel, shards), (outer_attn, moment_attn), [(piece, f32)] * 2,
        [pltpu.VMEM((2, outer_attn.shape[1], 2 * LANES), f32)],
    )
    steps = []
    for n, masks in enumerate(hops(shards)):
        moved = hop(mine, *masks)
        if n == 0:
            moved = after(moved, outer_piece)
        if n == 2:
            send, delta = call(
                functools.partial(middle_kernel, shards), (after(outer_piece, steps[1]), moment_piece, inner_norms[0], got),
                [((2 * shards, ROWS, LANES), bf16), (piece, f32)], [pltpu.VMEM((8, LANES), f32)], here=(3,),
            )
            moved = after(moved, delta)
        mine = mine + moved
        steps.append(mine)
    other = swap_shards(mine, 1)

    replica = everyone(after(send, steps[2]))
    delta_other = swap_groups(delta)
    embed = chunks(rows)
    coeff = pl.pallas_call(
        functools.partial(join_kernel, 0.5 / math.sqrt(RANK * VOCAB)),
        out_shape=jax.ShapeDtypeStruct((3 * rank, width), bf16),
        in_specs=[pl.BlockSpec(memory_space=VMEM)] * 2,
        out_specs=pl.BlockSpec(memory_space=VMEM),
        compiler_params=pltpu.CompilerParams(vmem_limit_bytes=LIMIT),
        cost_estimate=cost(5 * 10**8, 16 * rank * width),
    )(mine, other)
    new_embed, new_moment_embed = call(
        functools.partial(embed_kernel, embed),
        (after(coeff, delta_other), basis, outer_embed, moment_embed), [((rows, width), f32)] * 2,
        flops=6 * rank * rows * width, parts={2: embed, 3: embed}, here=(0,), weight=18,
    )
    new_attn, new_moment_attn, new_norms, new_moment_norms = call(
        functools.partial(attn_kernel, shards),
        (delta, delta_other, outer_attn, moment_attn, outer_norms, moment_norms),
        [(outer_attn.shape, f32)] * 2 + [(outer_norms.shape, f32)] * 2,
        [pltpu.VMEM((outer_attn.shape[1], 2 * LANES), f32)], here=(1,),
    )
    (replica_attn,) = call(
        functools.partial(replica_kernel, shards), (replica,), [(inner_attn.shape[1:], bf16)], here=(0,)
    )
    return (new_embed, new_moment_embed, new_attn.T, new_moment_attn.T, new_norms, new_moment_norms, replica_attn)


def plain(
    inner_embed, outer_embed, moment_embed, basis, inner_attn, outer_attn, moment_attn,
    inner_norms, outer_norms, moment_norms,
):
    groups = lax.axis_size("group")
    coeff = lax.dot_general(
        basis, outer_embed - inner_embed[0], (((0,), (0,)), ((), ())),
        precision=lax.Precision.HIGHEST, preferred_element_type=f32,
    )
    moved = lax.all_to_all(inner_attn[0], "shard", split_axis=1, concat_axis=0, tiled=True)
    coeff = lax.psum(coeff, ("group", "shard")) / groups
    attn_sum, norm_sum = lax.psum((outer_attn - moved, outer_norms - inner_norms[0]), "group")
    embed_delta = jnp.dot(basis, coeff, precision=lax.Precision.HIGHEST, preferred_element_type=f32) * (
        1.0 / math.sqrt(RANK * VOCAB)
    )
    new_embed, new_moment_embed = nesterov(outer_embed, moment_embed, embed_delta)
    new_attn, new_moment_attn = nesterov(outer_attn, moment_attn, attn_sum / groups)
    new_norms, new_moment_norms = nesterov(outer_norms, moment_norms, norm_sum / groups)
    replica_attn = lax.all_to_all(new_attn.astype(bf16), "shard", split_axis=0, concat_axis=1, tiled=True)
    return (new_embed, new_moment_embed, new_attn, new_moment_attn, new_norms, new_moment_norms, replica_attn)


def on_device(*args):
    outer_embed, basis, inner_attn, outer_attn, norms = args[1], args[3], args[4], args[5], args[8]
    shards = lax.axis_size("shard")
    fits = (
        lax.axis_size("group") == 2
        and shards >= 2
        and shards & (shards - 1) == 0
        and inner_attn.shape == (1, 48, 192 * shards)
        and outer_attn.shape == (48 * shards, 192)
        and outer_attn.shape[0] % LANES == 0
        and shards % 4 == 0
        and norms.shape[0] <= 8
        and norms.shape[1] <= HALF
        and outer_embed.shape[1] % 256 == 0
        and outer_embed.shape[0] % 8 == 0
        and basis.shape[1] % 16 == 0
    )
    return (fast if fits else plain)(*args)


def solution(mesh):
    placed = (
        P("group", "shard", None),
        P("shard", None),
        P("shard", None),
        P("shard", None),
        P("group", "shard", None),
        P(None, "shard"),
        P(None, "shard"),
        P("group", None, "shard"),
        P(None, "shard"),
        P(None, "shard"),
    )
    return jax.shard_map(
        on_device,
        mesh=mesh,
        in_specs=placed,
        out_specs=(
            P("shard", None),
            P("shard", None),
            P(None, "shard"),
            P(None, "shard"),
            P(None, "shard"),
            P(None, "shard"),
            P("shard", None),
        ),
        check_vma=False,
    )
```
